32 devices in a mesh: dp: 4 (over y, core), seq: 8 (over z, x).
Axes of the slice: x: 2, y: 2, z: 4, core: 2. Of those that a mesh axis runs over, the one named last changes fastest.
Arguments:
- queries: bfloat16 [8192, 4096], P(('dp', 'seq')), parts along dimension 0, may hold values from -6 to 6
- keys: bfloat16 [8192, 1024], P(('dp', 'seq')), parts along dimension 0, may hold values from -6 to 6
- values: bfloat16 [8192, 1024], P(('dp', 'seq')), parts along dimension 0, may hold values from -6 to 6
- lengths: int32 [32], P('dp'), parts along dimension 0, may hold values from 1 to 1024, 2048 in all
- span_order: int32 [128], P('dp'), parts along dimension 0, may hold values from 0 to 31, each once
Outputs:
- attended: bfloat16 [8192, 4096], P(('dp', 'seq')), parts along dimension 0
The draws below stay inside these ranges and needn't reach their ends.
There are 4 independent parts, one for each index of `dp`. The reference program is written for one: setup_inputs(seed, part) draws one part's arguments, and reference() takes and returns one part's arrays. A program takes and returns all parts, laid end to end along the dimension named above; each array names one. Nothing has to cross between parts.
Inputs may be any that keep to these rules, and one draw needn't show every extreme that they name: The lengths of one packed sequence sum to 2048; the longest is exactly 1024. A permutation of the 32 spans: balanced row b * 64 + i holds loader token span_order[b] * 64 + i.
All inputs are finite; a program needn't handle non-finite values.
Results may differ from the reference program's by a relative error of at most 0.0034.
Values may be sent and summed in bfloat16 or wider, within the bound.
No kernel may reach another device: no remote copies, remote signals or barrier semaphores. Data moves between devices by JAX's collectives and lax.ppermute only.
A program may use at most 64 MiB of HBM per device.

```python
import math
import jax
import jax.numpy as jnp
import numpy as np
from jax import lax

HEADS = 32
KV_HEADS = 8
HEAD_DIM = 128
BLOCK = 64
DOC_MOST = 1024
QBLOCK = 512
TOKENS = 2048
NDOC = 8
NCHUNK = 32


def draw_queries(key, part):
    width = HEADS * HEAD_DIM
    drawn = jnp.clip(jax.random.normal(jax.random.fold_in(key, 1), (TOKENS, width), jnp.float32), -4.0, 4.0)
    return drawn.astype(jnp.bfloat16)


def draw_keys(key, part):
    width = KV_HEADS * HEAD_DIM
    drawn = jnp.clip(jax.random.normal(jax.random.fold_in(key, 2), (TOKENS, width), jnp.float32), -4.0, 4.0)
    return drawn.astype(jnp.bfloat16)


def steps_of(stream_key, extent, cuts, least, top_value):
    def one(axis_at, blocks):
        steps = jax.random.uniform(jax.random.fold_in(jax.random.fold_in(stream_key, 6), axis_at), (blocks,), jnp.float32, least / len(cuts), top_value / len(cuts))
        return jnp.repeat(jnp.exp(steps), extent[axis_at] // blocks).reshape((-1,) + (1,) * (len(extent) - axis_at - 1))

    level = one(*cuts[0])
    for cut in cuts[1:]:
        level = level * one(*cut)
    return level


def split_up(number_of, total, limit, skew):
    weights = [(1 << 20) // math.isqrt(rank ** skew) + 1 for rank in range(2, number_of + 1)]
    surplus, counts = total - limit - (number_of - 1), [1] * (number_of - 1)
    while surplus > 0:
        movable = [i for i in range(number_of - 1) if counts[i] < limit]
        pool, remaining = sum([weights[i] for i in movable]), surplus
        for i in movable:
            addition = min(limit - counts[i], max(1, remaining * weights[i] // pool), surplus)
            counts[i] = counts[i] + addition
            surplus = surplus - addition
    return np.array([limit] + counts)


def ragged(key, number_of, total, limit, lean):
    if number_of == 2:
        one = jax.random.randint(key, (), max(1, total - limit), min(limit, total - 1) + 1)
        return jnp.stack([one, total - one])
    tallies = jnp.asarray(split_up(number_of, total, limit, lean), jnp.int32)
    couples = (number_of - 1) // 2
    donor, receiver = tallies[1:1 + 2 * couples:2], tallies[2:2 + 2 * couples:2]
    room = jnp.minimum(donor - 1, limit - receiver)
    passed = jax.random.randint(jax.random.fold_in(key, 1), (couples,), 0, 1 << 20) % (room + 1)
    tallies = tallies.at[1:1 + 2 * couples:2].set(donor - passed).at[2:2 + 2 * couples:2].set(receiver + passed)
    return tallies[jax.random.permutation(jax.random.fold_in(key, 2), number_of)]


def gaussian(stream_key, shape, spread, reach, shards=(), kind=jnp.bfloat16):
    entries = spread * jax.random.normal(stream_key, shape, jnp.float32)
    if shards:
        entries = entries * steps_of(stream_key, shape, shards, -0.22, 0.18)
    return jnp.clip(entries, -reach, reach).astype(kind)


def setup_inputs(seed: int = 0, part: int = 0) -> dict:
    seeds = jax.random.split(jax.random.key(seed), 6)
    own_keys = jax.random.split(jax.random.fold_in(seeds[5], part), 6)
    queries = draw_queries(jax.random.fold_in(jax.random.fold_in(seeds[5], part), 71), part)
    keys = draw_keys(jax.random.fold_in(jax.random.fold_in(seeds[5], part), 71), part)
    values = gaussian(own_keys[2], (TOKENS, KV_HEADS * HEAD_DIM), 1.0, 6.0, ((0, 8),))
    lengths = ragged(own_keys[3], NDOC, TOKENS, DOC_MOST, 1).astype(jnp.int32)
    span_order = jax.random.permutation(own_keys[4], NCHUNK).astype(jnp.int32)
    return {"queries": queries, "keys": keys, "values": values, "lengths": lengths, "span_order": span_order}


def doc_numbers(lengths, places):
    doc_ends = jnp.cumsum(lengths.astype(jnp.int32))
    return jnp.sum((doc_ends[None, :] <= places[:, None]).astype(jnp.int32), axis=1)


def band_attention(query_group, key_rows, value_rows, doc_ids):
    total_rows = query_group.shape[0]
    group_size = query_group.shape[1]
    pad_keys = jnp.concatenate([jnp.zeros((DOC_MOST, HEAD_DIM), key_rows.dtype), key_rows], 0)
    pad_values = jnp.concatenate([jnp.zeros((DOC_MOST, HEAD_DIM), value_rows.dtype), value_rows], 0)
    pad_docs = jnp.concatenate([jnp.full((DOC_MOST,), -1, jnp.int32), doc_ids.astype(jnp.int32)], 0)
    scale_factor = HEAD_DIM ** -0.5

    def one_block(block_index):
        row_start = (block_index * QBLOCK).astype(jnp.int32)
        query_block = lax.dynamic_slice_in_dim(query_group, row_start, QBLOCK, 0)
        key_block = lax.dynamic_slice_in_dim(pad_keys, row_start, QBLOCK + DOC_MOST, 0)
        value_block = lax.dynamic_slice_in_dim(pad_values, row_start, QBLOCK + DOC_MOST, 0)
        query_docs = lax.dynamic_slice_in_dim(pad_docs, row_start + DOC_MOST, QBLOCK, 0)
        key_docs = lax.dynamic_slice_in_dim(pad_docs, row_start, QBLOCK + DOC_MOST, 0)
        query_pos = row_start + jnp.arange(QBLOCK, dtype=jnp.int32)
        key_pos = row_start - DOC_MOST + jnp.arange(QBLOCK + DOC_MOST, dtype=jnp.int32)
        allowed = (query_docs[:, None] == key_docs[None, :]) & (key_pos[None, :] <= query_pos[:, None])
        scores = jnp.einsum("qgd,kd->gqk", query_block.astype(jnp.float32), key_block.astype(jnp.float32)) * scale_factor
        scores = jnp.where(allowed[None], scores, -jnp.inf)
        row_top = jnp.max(scores, axis=-1, keepdims=True)
        weights = jnp.exp(scores - row_top)
        row_total = jnp.sum(weights, axis=-1, keepdims=True)
        rounded = lax.optimization_barrier(weights.astype(jnp.bfloat16))
        mixed_rows = jnp.einsum("gqk,kd->qgd", rounded.astype(jnp.float32), value_block.astype(jnp.float32))
        return (mixed_rows / jnp.transpose(row_total, (1, 0, 2))).astype(jnp.bfloat16)

    blocks = lax.map(one_block, jnp.arange(total_rows // QBLOCK, dtype=jnp.int32))
    return blocks.reshape(total_rows, group_size * HEAD_DIM)


def reference(queries, keys, values, lengths, span_order):
    total_rows = queries.shape[0]
    nchunk = span_order.shape[0]
    inverse = jnp.zeros((nchunk,), jnp.int32).at[span_order].set(jnp.arange(nchunk, dtype=jnp.int32))
    places = jnp.arange(total_rows, dtype=jnp.int32)
    doc_ids = doc_numbers(lengths, places)

    def to_loader(array):
        return array.reshape(nchunk, BLOCK, -1)[inverse].reshape(total_rows, -1)

    loader_queries = to_loader(queries)
    loader_keys = to_loader(keys)
    loader_values = to_loader(values)
    group_size = HEADS // KV_HEADS

    def per_kv(kv_index):
        query_group = lax.dynamic_slice_in_dim(loader_queries, kv_index * group_size * HEAD_DIM, group_size * HEAD_DIM, 1)
        query_group = query_group.reshape(total_rows, group_size, HEAD_DIM)
        key_rows = lax.dynamic_slice_in_dim(loader_keys, kv_index * HEAD_DIM, HEAD_DIM, 1)
        value_rows = lax.dynamic_slice_in_dim(loader_values, kv_index * HEAD_DIM, HEAD_DIM, 1)
        return band_attention(query_group, key_rows, value_rows, doc_ids)

    group_outputs = lax.map(per_kv, jnp.arange(KV_HEADS, dtype=jnp.int32))
    loader_out = jnp.transpose(group_outputs, (1, 0, 2)).reshape(total_rows, HEADS * HEAD_DIM)
    return loader_out.reshape(nchunk, BLOCK, -1)[span_order].reshape(total_rows, -1)
```

```python
import math
import jax
import jax.numpy as jnp
from jax import lax
from jax.experimental import pallas as pl
from jax.experimental.pallas import tpu as pltpu
from jax.sharding import PartitionSpec as P

HEADS = 32
KV_HEADS = 8
HEAD_DIM = 128
BLOCK = 64
DOC_MOST = 1024
GROUP = HEADS // KV_HEADS
KEY_STEP = 128
MOST_STEPS = -(-(DOC_MOST + BLOCK) // KEY_STEP)
CHUNKS = 2
KV_CHUNK = KV_HEADS // 2 // CHUNKS
Q_CHUNK = KV_CHUNK * GROUP
PAD = 128
EXP_SCALE = HEAD_DIM**-0.5 * math.log2(math.e)


def attend_span(lengths, row0, load_q, store_out, kv):
    row = row0 + lax.broadcasted_iota(jnp.int32, (BLOCK, KEY_STEP), 0)
    low = jnp.int32(0)
    starts = jnp.zeros((BLOCK, KEY_STEP), jnp.int32)
    end = jnp.int32(0)
    for j in range(lengths.shape[0]):
        end = end + lengths[j]
        low = jnp.where(end <= row0, end, low)
        starts = jnp.where(end <= row, end, starts)
    first = pl.multiple_of((low // BLOCK) * BLOCK, BLOCK)
    steps = (row0 + BLOCK - first + KEY_STEP - 1) // KEY_STEP

    def variant(count):
        width = count * KEY_STEP
        biases = []
        for t in range(count):
            col = first + t * KEY_STEP + lax.broadcasted_iota(jnp.int32, (BLOCK, KEY_STEP), 1)
            biases.append(jnp.where((col >= starts) & (col <= row), 0.0, -1e30).astype(jnp.float32))
        bias = jnp.concatenate(biases, axis=1)
        bias = jnp.concatenate([bias] * GROUP, axis=0)
        ones = jnp.ones((width, HEAD_DIM), jnp.bfloat16)
        for g in range(KV_CHUNK):
            q = load_q(g)
            k = kv[pl.ds(first, width), g * HEAD_DIM : (g + 1) * HEAD_DIM]
            v = kv[pl.ds(first, width), (KV_CHUNK + g) * HEAD_DIM : (KV_CHUNK + g + 1) * HEAD_DIM]
            s = lax.dot_general(q, k, (((1,), (1,)), ((), ())), preferred_element_type=jnp.float32)
            s = s + bias
            top = jnp.max(s, axis=1, keepdims=True)
            p = jnp.exp2((s - top) * EXP_SCALE).astype(jnp.bfloat16)
            mixed = jnp.dot(p, jnp.concatenate([v, ones], axis=1), preferred_element_type=jnp.float32)
            store_out(g, (mixed[:, :HEAD_DIM] / mixed[:, HEAD_DIM:]).astype(jnp.bfloat16))

    for count in range(1, MOST_STEPS + 1):
        pl.when(steps == count)(lambda count=count: variant(count))


def attention_kernel(seq_devices, lengths, order, q_own, q_pair, *rest):
    line = seq_devices // 2
    shards = rest[: 2 * line - 1]
    out_own, out_pair, kv, sem = rest[2 * line - 1 :]
    spans = q_own.shape[0] // BLOCK
    total_rows = order.shape[0] * BLOCK
    me = lax.axis_index("seq")
    place = me // 2
    pair = me - 2 * place

    def copies(ref, owner_place):
        for half in range(2):
            owner = 2 * owner_place + (pair if half == 0 else 1 - pair)
            for t in range(spans):
                target = pl.multiple_of(order[owner * spans + t] * BLOCK, BLOCK)
                yield pltpu.make_async_copy(
                    ref.at[pl.ds((half * spans + t) * BLOCK, BLOCK), :], kv.at[pl.ds(target, BLOCK), :], sem
                )

    def each(action):
        def act(ref, owner_place):
            for copy in copies(ref, owner_place):
                action(copy)

        act(shards[0], place)
        for k in range(1, line):
            pl.when(place >= k)(lambda k=k: act(shards[k], place - k))
            pl.when(place < k)(lambda k=k: act(shards[line - 1 + line - k], place - k + line))

    each(lambda copy: copy.start())
    kv[pl.ds(total_rows, PAD), :] = jnp.zeros((PAD, kv.shape[1]), jnp.bfloat16)
    each(lambda copy: copy.wait())

    for half, (q_ref, out_ref) in enumerate(((q_own, out_own), (q_pair, out_pair))):
        owner = me if half == 0 else 2 * place + 1 - pair

        def one_span(i, carry, q_ref=q_ref, out_ref=out_ref, owner=owner):
            rows = pl.ds(pl.multiple_of(i * BLOCK, BLOCK), BLOCK)

            def load_q(g):
                return jnp.concatenate(
                    [q_ref[rows, (g * GROUP + j) * HEAD_DIM : (g * GROUP + j + 1) * HEAD_DIM] for j in range(GROUP)], axis=0
                )

            def store_out(g, o):
                for j in range(GROUP):
                    out_ref[rows, (g * GROUP + j) * HEAD_DIM : (g * GROUP + j + 1) * HEAD_DIM] = o[
                        j * BLOCK : (j + 1) * BLOCK
                    ]

            attend_span(lengths, order[owner * spans + i] * BLOCK, load_q, store_out, kv)
            return carry

        lax.fori_loop(0, spans, one_span, 0)


def attention(seq_devices, lengths, order, q_own, q_pair, shards):
    total_rows = order.shape[0] * BLOCK
    out = jax.ShapeDtypeStruct(q_own.shape, jnp.bfloat16)
    smem = pl.BlockSpec(memory_space=pltpu.SMEM)
    vmem = pl.BlockSpec(memory_space=pltpu.VMEM)
    hbm = pl.BlockSpec(memory_space=pl.ANY)
    pairs = 2 * q_own.shape[0] * Q_CHUNK * 600
    return pl.pallas_call(
        lambda *refs: attention_kernel(seq_devices, *refs),
        out_shape=(out, out),
        in_specs=[smem, smem, vmem, vmem] + [hbm] * len(shards),
        out_specs=(vmem, vmem),
        scratch_shapes=[
            pltpu.VMEM((total_rows + PAD, 2 * KV_CHUNK * HEAD_DIM), jnp.bfloat16),
            pltpu.SemaphoreType.DMA,
        ],
        compiler_params=pltpu.CompilerParams(vmem_limit_bytes=40 * 1024 * 1024),
        cost_estimate=pl.CostEstimate(
            flops=pairs * 4 * HEAD_DIM, bytes_accessed=4 * q_own.size * 2 + total_rows * 1024, transcendentals=pairs
        ),
        name="attention",
    )(lengths, order, q_own, q_pair, *shards)


def shards(queries, keys, values, lengths, order):
    seq_devices = lax.axis_size("seq")
    line = seq_devices // 2
    me = lax.axis_index("seq")
    pair = me % 2
    swap = [(i, i ^ 1) for i in range(seq_devices)]
    kv_half = KV_HEADS // 2 * HEAD_DIM
    q_half = HEADS // 2 * HEAD_DIM

    def columns(array, half, width, chunk, size):
        return lax.dynamic_slice_in_dim(array, half * width + chunk * size, size, 1)

    def kv_piece(half, chunk):
        size = KV_CHUNK * HEAD_DIM
        return jnp.concatenate(
            [columns(keys, half, kv_half, chunk, size), columns(values, half, kv_half, chunk, size)], axis=1
        )

    def gather(shard):
        right, left = [], []
        r = l = shard
        for k in range(1, line):
            r = lax.ppermute(r, "seq", [(2 * z + x, 2 * z + 2 + x) for z in range(k - 1, line - 1) for x in range(2)])
            l = lax.ppermute(l, "seq", [(2 * z + x, 2 * z - 2 + x) for z in range(1, line + 1 - k) for x in range(2)])
            right.append(r)
            left.append(l)
        return [shard] + right + left

    gathered, q_owns, q_pairs = [], [], []
    size = Q_CHUNK * HEAD_DIM
    for c in range(CHUNKS):
        got = lax.ppermute(kv_piece(1 - pair, c), "seq", swap)
        gathered.append(gather(jnp.concatenate([kv_piece(pair, c), got], axis=0)))
    for c in range(CHUNKS):
        q_owns.append(columns(queries, pair, q_half, c, size))
        q_pairs.append(lax.ppermute(columns(queries, 1 - pair, q_half, c, size), "seq", swap))
    mine, theirs = [], []
    for c in range(CHUNKS):
        own, other = attention(seq_devices, lengths, order, q_owns[c], q_pairs[c], gathered[c])
        mine.append(own)
        theirs.append(lax.ppermute(other, "seq", swap))
    mine, theirs = jnp.concatenate(mine, axis=1), jnp.concatenate(theirs, axis=1)
    return jnp.where(
        pair == 0, jnp.concatenate([mine, theirs], axis=1), jnp.concatenate([theirs, mine], axis=1)
    )


def solution(mesh):
    placed = (
        P(("dp", "seq"), None),
        P(("dp", "seq"), None),
        P(("dp", "seq"), None),
        P("dp"),
        P("dp"),
    )
    return jax.shard_map(
        shards, mesh=mesh, in_specs=placed, out_specs=P(("dp", "seq"), None), check_vma=False
    )
```

```python
import math
import jax
import jax.numpy as jnp
from jax import lax
from jax.experimental import pallas as pl
from jax.experimental.pallas import tpu as pltpu
from jax.sharding import PartitionSpec as P

HEADS = 32
KV_HEADS = 8
HEAD_DIM = 128
BLOCK = 64
DOC_MOST = 1024
GROUP = HEADS // KV_HEADS
KV_HALF = KV_HEADS // 2
KEY_STEP = 128
MOST_STEPS = -(-(DOC_MOST + BLOCK) // KEY_STEP)
EXP_SCALE = HEAD_DIM**-0.5 * math.log2(math.e)
GQ = GROUP * HEAD_DIM
VMEM_BYTES = 60 * 1024 * 1024
COUNTS = tuple(range(1, MOST_STEPS + 1))
TOGETHER = {1: 2, 2: 2}


def attend_spans(lengths, positions, heads, load_q, store_out, kv):
    spans = []
    most = jnp.int32(0)
    for row0 in positions:
        row = row0 + lax.broadcasted_iota(jnp.int32, (BLOCK, KEY_STEP), 0)
        low = jnp.int32(0)
        starts = jnp.zeros((BLOCK, KEY_STEP), jnp.int32)
        end = jnp.int32(0)
        for j in range(lengths.shape[0]):
            end = end + lengths[j]
            low = jnp.where(end <= row0, end, low)
            starts = jnp.where(end <= row, end, starts)
        spans.append((row0, row, starts))
        most = jnp.maximum(most, row0 + BLOCK - (low // BLOCK) * BLOCK)
    steps = (most + KEY_STEP - 1) // KEY_STEP

    def variant(count):
        width = count * KEY_STEP
        tiles = []
        for u, (row0, row, starts) in enumerate(spans):
            first = pl.multiple_of(jnp.maximum(row0 + BLOCK - width, 0), BLOCK)
            biases = []
            for t in range(count):
                col = first + t * KEY_STEP + lax.broadcasted_iota(jnp.int32, (BLOCK, KEY_STEP), 1)
                biases.append(jnp.where((col >= starts) & (col <= row), 0.0, -1e30).astype(jnp.float32))
            bias = jnp.concatenate(biases, axis=1)
            bias = jnp.concatenate([bias] * GROUP, axis=0)
            for g in range(heads):
                k = kv[pl.ds(first, width), g * HEAD_DIM : (g + 1) * HEAD_DIM]
                s = lax.dot_general(load_q(u, g), k, (((1,), (1,)), ((), ())), preferred_element_type=jnp.float32)
                tiles.append((u, g, first, s + bias))
        for u, g, first, s in tiles:
            v = kv[pl.ds(first, width), (heads + g) * HEAD_DIM : (heads + g + 1) * HEAD_DIM]
            top = jnp.max(s, axis=1, keepdims=True)
            p = jnp.exp2((s - top) * EXP_SCALE)
            total = jnp.sum(p, axis=1, keepdims=True)
            mixed = jnp.dot(p.astype(jnp.bfloat16), v, preferred_element_type=jnp.float32)
            store_out(u, g, (mixed / total).astype(jnp.bfloat16))

    def choose(counts):
        if len(counts) == 1:
            variant(counts[0])
            return
        half = len(counts) // 2
        small = steps <= counts[half - 1]
        pl.when(small)(lambda: choose(counts[:half]))
        pl.when(jnp.logical_not(small))(lambda: choose(counts[half:]))

    choose(COUNTS)


def attention(name, heads, lengths, order, arrays, q_plan, kv_plan, active=None, wide=None, column=None):
    total_rows = order.shape[0] * BLOCK
    rows_here = total_rows // lax.axis_size("seq")
    spans = rows_here // BLOCK
    q_width, kv_width = heads * GQ, 2 * heads * HEAD_DIM
    blocks = len(q_plan(0, 0))
    together = TOGETHER[heads]

    def kernel(lengths, order, *refs):
        inputs, outs = refs[: len(arrays)], refs[-5 - blocks : -5]
        kv, q_all, o_all, sem_in, sem_out = refs[-5:]
        me = lax.axis_index("seq")
        place = me // 2
        pair = me - 2 * place
        queries = q_plan(place, pair)

        def q_copy(b):
            array, row, column, _ = queries[b]
            return pltpu.make_async_copy(
                inputs[array].at[pl.ds(row, rows_here), pl.ds(column, q_width)],
                q_all.at[pl.ds(b * rows_here, rows_here), :],
                sem_in,
            )

        def out_copy(b, i):
            source = pl.multiple_of(b * rows_here + i * BLOCK, BLOCK)
            target = pl.multiple_of(i * BLOCK, BLOCK)
            size = together * BLOCK
            place = outs[b].at[pl.ds(target, size), :]
            if column is not None and b == blocks - 1:
                place = outs[b].at[pl.ds(target, size), pl.ds(column(pair), q_width)]
            return pltpu.make_async_copy(
                o_all.at[pl.ds(source, size), :], place, sem_out
            )

        def each_kv(action):
            for condition, array, row, column, owner in kv_plan(place, pair):

                def act(array=array, row=row, column=column, owner=owner):
                    for t in range(spans):
                        target = pl.multiple_of(order[owner * spans + t] * BLOCK, BLOCK)
                        action(
                            pltpu.make_async_copy(
                                inputs[array].at[pl.ds(row + t * BLOCK, BLOCK), pl.ds(column, kv_width)],
                                kv.at[pl.ds(target, BLOCK), :],
                                sem_in,
                            )
                        )

                act() if condition is None else pl.when(condition)(act)

        def one_group(i, carry):
            block = i * together // spans
            owner = queries[0][3]
            for b in range(1, blocks):
                owner = jnp.where(block == b, queries[b][3], owner)
            within = i * together - block * spans

            def rows(u):
                return pl.ds(pl.multiple_of((i * together + u) * BLOCK, BLOCK), BLOCK)

            def load_q(u, g):
                return jnp.concatenate(
                    [q_all[rows(u), (g * GROUP + j) * HEAD_DIM : (g * GROUP + j + 1) * HEAD_DIM] for j in range(GROUP)],
                    axis=0,
                )

            def store_out(u, g, o):
                for j in range(GROUP):
                    o_all[rows(u), (g * GROUP + j) * HEAD_DIM : (g * GROUP + j + 1) * HEAD_DIM] = o[
                        j * BLOCK : (j + 1) * BLOCK
                    ]

            positions = [order[owner * spans + within + u] * BLOCK for u in range(together)]
            attend_spans(lengths, positions, heads, load_q, store_out, kv)
            for b in range(blocks):
                pl.when(block == b)(lambda b=b: out_copy(b, within).start())
            return carry

        def body():
            each_kv(lambda copy: copy.start())
            for b in range(blocks):
                q_copy(b).start()
            pltpu.make_async_copy(kv.at[pl.ds(0, total_rows), :], kv.at[pl.ds(0, total_rows), :], sem_in).wait()
            for b in range(blocks):
                q_copy(b).wait()
            lax.fori_loop(0, blocks * spans // together, one_group, 0)
            for b in range(blocks):
                for i in range(0, spans, together):
                    out_copy(b, i).wait()

        body() if active is None else pl.when(active(place))(body)

    smem = pl.BlockSpec(memory_space=pltpu.SMEM)
    hbm = pl.BlockSpec(memory_space=pl.ANY)
    pairs = blocks * rows_here * heads * GROUP * 600
    shapes = [jax.ShapeDtypeStruct((rows_here, q_width), jnp.bfloat16)] * blocks
    if column is not None:
        shapes[-1] = jax.ShapeDtypeStruct((rows_here, HEADS * HEAD_DIM), jnp.bfloat16)
    given = [] if wide is None else [wide]
    return pl.pallas_call(
        kernel,
        out_shape=shapes,
        in_specs=[smem, smem] + [hbm] * (len(arrays) + len(given)),
        out_specs=[hbm] * blocks,
        scratch_shapes=[
            pltpu.VMEM((total_rows, kv_width), jnp.bfloat16),
            pltpu.VMEM((blocks * rows_here, q_width), jnp.bfloat16),
            pltpu.VMEM((blocks * rows_here, q_width), jnp.bfloat16),
            pltpu.SemaphoreType.DMA,
            pltpu.SemaphoreType.DMA,
        ],
        compiler_params=pltpu.CompilerParams(vmem_limit_bytes=VMEM_BYTES),
        cost_estimate=pl.CostEstimate(
            flops=pairs * 4 * HEAD_DIM, bytes_accessed=4 * blocks * rows_here * q_width, transcendentals=pairs
        ),
        input_output_aliases={2 + len(arrays): blocks - 1} if given else {},
        name=name,
    )(lengths, order, *arrays, *given)


def split(name, arrays, widths, plan):
    n, count = arrays[0].shape[0], len(widths)

    def kernel(*refs):
        inputs, outs = refs[: len(arrays)], refs[len(arrays) : len(arrays) + count]
        held, sems, sem_out = refs[len(arrays) + count : -2], refs[-2], refs[-1]
        pair = lax.axis_index("seq") % 2

        def ins(o):
            to = 0
            for array, first, size in plan(pair)[o]:
                yield pltpu.make_async_copy(
                    inputs[array].at[:, pl.ds(first, size)], held[o].at[:, pl.ds(to, size)], sems.at[o]
                )
                to += size

        for o in range(count):
            for copy in ins(o):
                copy.start()
        for o in range(count):
            for copy in ins(o):
                copy.wait()
            pltpu.make_async_copy(held[o], outs[o], sem_out).start()
        for o in range(count):
            pltpu.make_async_copy(held[o], outs[o], sem_out).wait()

    hbm = pl.BlockSpec(memory_space=pl.ANY)
    return pl.pallas_call(
        kernel,
        out_shape=[jax.ShapeDtypeStruct((n, width), jnp.bfloat16) for width in widths],
        in_specs=[hbm] * len(arrays),
        out_specs=[hbm] * count,
        scratch_shapes=[pltpu.VMEM((n, width), jnp.bfloat16) for width in widths]
        + [pltpu.SemaphoreType.DMA((count,)), pltpu.SemaphoreType.DMA],
        compiler_params=pltpu.CompilerParams(vmem_limit_bytes=VMEM_BYTES),
        cost_estimate=pl.CostEstimate(flops=0, bytes_accessed=4 * n * sum(widths), transcendentals=0),
        name=name,
    )(*arrays)


def columns(array, first, size):
    return lax.dynamic_slice_in_dim(array, first, size, 1)


def kv_columns(keys, values, half, head, count):
    first, size = (half * KV_HALF + head) * HEAD_DIM, count * HEAD_DIM
    return [columns(keys, first, size), columns(values, first, size)]


def assemble(pair, mine, theirs):
    mine, theirs = jnp.concatenate(mine, axis=1), jnp.concatenate(theirs, axis=1)
    return jnp.where(
        pair == 0, jnp.concatenate([mine, theirs], axis=1), jnp.concatenate([theirs, mine], axis=1)
    )


def line_shards(queries, keys, values, lengths, order):
    devices = lax.axis_size("seq")
    line = devices // 2
    pair = lax.axis_index("seq") % 2
    rows_here = queries.shape[0]
    swap = [(i, i ^ 1) for i in range(devices)]

    def gather(shard):
        right, left = [], []
        r = l = shard
        for k in range(1, line):
            r = lax.ppermute(r, "seq", [(2 * z + x, 2 * z + 2 + x) for z in range(k - 1, line - 1) for x in range(2)])
            l = lax.ppermute(l, "seq", [(2 * z + x, 2 * z - 2 + x) for z in range(1, line + 1 - k) for x in range(2)])
            right.append(r)
            left.append(l)
        return [shard] + right + left

    mine, theirs = [], []
    heads = KV_HALF // 2
    for c in range(2):
        own = jnp.concatenate(kv_columns(keys, values, pair, c * heads, heads), axis=1)
        other = jnp.concatenate(kv_columns(keys, values, 1 - pair, c * heads, heads), axis=1)
        gathered = gather(jnp.concatenate([own, lax.ppermute(other, "seq", swap)], axis=0))
        q_other = lax.ppermute(
            columns(queries, (1 - pair) * KV_HALF * GQ + c * heads * GQ, heads * GQ), "seq", swap
        )

        def q_plan(place, pair, c=c):
            me = 2 * place + pair
            return [(0, 0, pair * KV_HALF * GQ + c * heads * GQ, me), (1, 0, 0, 2 * place + 1 - pair)]

        def kv_plan(place, pair):
            plan = []
            for half, x in enumerate((pair, 1 - pair)):
                row = half * rows_here
                plan.append((None, 2, row, 0, 2 * place + x))
                for k in range(1, line):
                    plan.append((place >= k, 2 + k, row, 0, 2 * (place - k) + x))
                    plan.append((place < k, 2 + line - 1 + line - k, row, 0, 2 * (place - k + line) + x))
            return plan

        a, b = attention("attention", heads, lengths, order, [queries, q_other] + gathered, q_plan, kv_plan)
        mine.append(a)
        theirs.append(lax.ppermute(b, "seq", swap))
    return assemble(pair, mine, theirs)


def after(array, *others):
    return lax.optimization_barrier((array,) + others)[0]


def short_shards(queries, keys, values, lengths, order):
    pair = lax.axis_index("seq") % 2
    n = queries.shape[0]
    parts = lax.axis_size("dp")
    both = ("dp", "seq")

    def permutation(links):
        return [(8 * d + 2 * a + x, 8 * d + 2 * b + x) for d in range(parts) for a, b in links for x in range(2)]

    outer = permutation([(0, 1), (1, 0), (2, 3), (3, 2)])
    inner = permutation([(1, 2), (2, 1)])
    inner += [(8 * d + 2 * z + x, 8 * (d ^ 1) + 2 * z + x) for d in range(parts) for z in (0, 3) for x in range(2)]
    across = [(8 * d + i, 8 * d + (i ^ 1)) for d in range(parts) for i in range(8)]

    def swap_x(a):
        return lax.ppermute(a, both, across)

    def swap_outer(a):
        return lax.ppermute(a, both, outer)

    def swap_inner(a):
        return lax.ppermute(a, both, inner)

    def rows(*blocks):
        return jnp.concatenate(blocks, axis=0)

    def middle(place):
        return (place == 1) | (place == 2)

    def end(place):
        return jnp.logical_not(middle(place))

    def near(place):
        return place + 1 - 2 * (place % 2)

    one, two = HEAD_DIM, 2 * HEAD_DIM
    kv_half, q_half = KV_HALF * HEAD_DIM, KV_HALF * GQ

    def t_plan(pair):
        return [[(a, half * kv_half, two) for a in range(2)] for half in (pair, 1 - pair)]

    def w_plan(pair):
        return [
            [(a, half * kv_half + head * one, one) for head in (2, 3) for a in range(2)] for half in (pair, 1 - pair)
        ]

    def q_plan(pair):
        return [[(0, (1 - pair) * q_half + i * 2 * GQ, 2 * GQ)] for i in range(2)]

    t_own, t_send = split("split_t", [keys, values], [2 * two] * 2, t_plan)
    t_par = swap_x(t_send)
    t_near_own = swap_outer(t_own)
    t_in_own = swap_inner(t_own)
    w_own, w_send = split("split_w", [keys, after(values, t_own)], [2 * two] * 2, w_plan)
    w_par = swap_x(w_send)
    qt_send, qw_send = split("split_q", [after(queries, w_own)], [2 * GQ] * 2, q_plan)
    t_near_par = swap_outer(t_par)
    t_in_par = swap_inner(t_par)
    w_shard = rows(w_own, w_par)
    qt_par = swap_x(after(qt_send, w_par))
    t_far_own = swap_inner(t_near_own)
    t_out_own = swap_outer(t_in_own)
    t_far_par = swap_inner(t_near_par)
    t_out_par = swap_outer(t_in_par)
    w_near = swap_outer(w_shard)
    w_in = swap_inner(w_shard)
    qw_par = swap_x(after(qw_send, qt_par))
    t_out_far_own = swap_outer(t_far_own)
    t_out_far_par = swap_outer(t_far_par)
    w_out = swap_outer(w_in)
    w_far = swap_inner(w_near)

    def each_half(plan):
        def full(place, pair):
            return [
                (condition, array, row, column, 2 * owner + x)
                for half, x in enumerate((pair, 1 - pair))
                for condition, array, row, column, owner in plan(place, half)
            ]

        return full

    def t_queries(place, pair):
        return [(1, 0, 0, 2 * place + 1 - pair), (0, 0, pair * q_half, 2 * place + pair)]

    def t_keys(place, half):
        return [
            (None, 2 + half, 0, 0, place),
            (None, 4 + half, 0, 0, near(place)),
            (middle(place), 6 + half, 0, 0, 3 - place),
            (middle(place), 8 + half, 0, 0, 3 - near(place)),
            (end(place), 10 + half, 0, 0, 3 - near(place)),
            (end(place), 12 + half, 0, 0, 3 - place),
        ]

    t_other, wide = attention(
        "attention_t",
        2,
        lengths,
        order,
        [queries, qt_par, t_own, t_par, t_near_own, t_near_par, t_in_own, t_in_par]
        + [t_far_own, t_far_par, t_out_own, t_out_par, t_out_far_own, t_out_far_par],
        t_queries,
        each_half(t_keys),
        column=lambda pair: pair * q_half,
    )
    t_theirs = swap_x(t_other)

    mine, theirs = pair * q_half, (1 - pair) * q_half
    blocks = [(t_theirs, theirs)]
    for head in (2, 3):
        first = (head - 2) * two
        far = swap_outer(w_far[:, first : first + two])

        def w_queries(place, pair, head=head):
            return [(1, 0, (head - 2) * GQ, 2 * place + 1 - pair), (0, 0, pair * q_half + head * GQ, 2 * place + pair)]

        def w_keys(place, half, first=first):
            return [
                (None, 2, half * n, first, place),
                (None, 3, half * n, first, near(place)),
                (middle(place), 4, half * n, first, 3 - place),
                (middle(place), 5, half * n, first, 3 - near(place)),
                (end(place), 6, half * n, first, 3 - near(place)),
                (end(place), 7, half * n, 0, 3 - place),
            ]

        other, wide = attention(
            "attention_" + str(head),
            1,
            lengths,
            order,
            [queries, qw_par, w_shard, w_near, w_in, w_far, w_out, far],
            w_queries,
            each_half(w_keys),
            wide=wide,
            column=lambda pair, head=head: pair * q_half + head * GQ,
        )
        blocks.append((swap_x(other), theirs + head * GQ))
    for block, column in blocks:
        wide = lax.dynamic_update_slice_in_dim(wide, block, column, 1)
    return wide


def shards(queries, keys, values, lengths, order):
    whole = short_shards if lax.axis_size("seq") == 8 else line_shards
    return whole(queries, keys, values, lengths, order)


def solution(mesh):
    placed = (
        P(("dp", "seq"), None),
        P(("dp", "seq"), None),
        P(("dp", "seq"), None),
        P("dp"),
        P("dp"),
    )
    return jax.shard_map(
        shards, mesh=mesh, in_specs=placed, out_specs=P(("dp", "seq"), None), check_vma=False
    )
```

```python
import math
import jax
import jax.numpy as jnp
from jax import lax
from jax.experimental import pallas as pl
from jax.experimental.pallas import tpu as pltpu
from jax.sharding import PartitionSpec as P

HEADS = 32
KV_HEADS = 8
HEAD_DIM = 128
BLOCK = 64
DOC_MOST = 1024
GROUP = HEADS // KV_HEADS
KV_HALF = KV_HEADS // 2
KEY_STEP = 128
MOST_STEPS = -(-(DOC_MOST + BLOCK) // KEY_STEP)
EXP_SCALE = HEAD_DIM**-0.5 * math.log2(math.e)
GQ = GROUP * HEAD_DIM
COST = {1: 0.3, 2: 1}
VMEM_BYTES = 60 * 1024 * 1024
WHOLE_VMEM = 64 * 1024 * 1024
COUNTS = (2, 4, 6, MOST_STEPS)
TOGETHER = {1: 2, 2: 2}


def attend_spans(lengths, positions, heads, load_q, store_out, kv):
    spans = []
    most = jnp.int32(0)
    for row0 in positions:
        row = row0 + lax.broadcasted_iota(jnp.int32, (BLOCK, KEY_STEP), 0)
        low = jnp.int32(0)
        starts = jnp.zeros((BLOCK, KEY_STEP), jnp.int32)
        end = jnp.int32(0)
        for j in range(lengths.shape[0]):
            end = end + lengths[j]
            low = jnp.where(end <= row0, end, low)
            starts = jnp.where(end <= row, end, starts)
        spans.append((row0, row, starts))
        most = jnp.maximum(most, row0 + BLOCK - (low // BLOCK) * BLOCK)
    steps = (most + KEY_STEP - 1) // KEY_STEP

    def variant(count):
        width = count * KEY_STEP
        tiles = []
        for u, (row0, row, starts) in enumerate(spans):
            first = pl.multiple_of(jnp.maximum(row0 + BLOCK - width, 0), BLOCK)
            biases = []
            for t in range(count):
                col = first + t * KEY_STEP + lax.broadcasted_iota(jnp.int32, (BLOCK, KEY_STEP), 1)
                biases.append(jnp.where((col >= starts) & (col <= row), 0.0, -1e30).astype(jnp.float32))
            bias = jnp.concatenate(biases, axis=1)
            bias = jnp.concatenate([bias] * GROUP, axis=0)
            for g in range(heads):
                k = kv[pl.ds(first, width), g * HEAD_DIM : (g + 1) * HEAD_DIM]
                s = lax.dot_general(load_q(u, g), k, (((1,), (1,)), ((), ())), preferred_element_type=jnp.float32)
                tiles.append((u, g, first, s + bias))
        for u, g, first, s in tiles:
            v = kv[pl.ds(first, width), (heads + g) * HEAD_DIM : (heads + g + 1) * HEAD_DIM]
            top = jnp.max(s, axis=1, keepdims=True)
            p = jnp.exp2((s - top) * EXP_SCALE)
            total = jnp.sum(p, axis=1, keepdims=True)
            mixed = jnp.dot(p.astype(jnp.bfloat16), v, preferred_element_type=jnp.float32)
            store_out(u, g, (mixed / total).astype(jnp.bfloat16))

    def choose(counts):
        if len(counts) == 1:
            variant(counts[0])
            return
        half = len(counts) // 2
        small = steps <= counts[half - 1]
        pl.when(small)(lambda: choose(counts[:half]))
        pl.when(jnp.logical_not(small))(lambda: choose(counts[half:]))

    choose(COUNTS)


def attention(name, heads, lengths, order, arrays, q_plan, kv_plan, active=None, wide=None, column=None):
    total_rows = order.shape[0] * BLOCK
    rows_here = total_rows // lax.axis_size("seq")
    spans = rows_here // BLOCK
    q_width, kv_width = heads * GQ, 2 * heads * HEAD_DIM
    blocks = len(q_plan(0, 0))
    together = TOGETHER[heads]

    def kernel(lengths, order, *refs):
        inputs, outs = refs[: len(arrays)], refs[-5 - blocks : -5]
        kv, q_all, o_all, sem_in, sem_out = refs[-5:]
        me = lax.axis_index("seq")
        place = me // 2
        pair = me - 2 * place
        queries = q_plan(place, pair)

        def q_copy(b):
            array, row, column, _ = queries[b]
            return pltpu.make_async_copy(
                inputs[array].at[pl.ds(row, rows_here), pl.ds(column, q_width)],
                q_all.at[pl.ds(b * rows_here, rows_here), :],
                sem_in,
            )

        def out_copy(b, i):
            source = pl.multiple_of(b * rows_here + i * BLOCK, BLOCK)
            target = pl.multiple_of(i * BLOCK, BLOCK)
            size = together * BLOCK
            place = outs[b].at[pl.ds(target, size), :]
            if column is not None and b == blocks - 1:
                place = outs[b].at[pl.ds(target, size), pl.ds(column(pair), q_width)]
            return pltpu.make_async_copy(
                o_all.at[pl.ds(source, size), :], place, sem_out
            )

        def each_kv(action):
            for condition, array, row, column, owner in kv_plan(place, pair):

                def act(array=array, row=row, column=column, owner=owner):
                    for t in range(spans):
                        target = pl.multiple_of(order[owner * spans + t] * BLOCK, BLOCK)
                        action(
                            pltpu.make_async_copy(
                                inputs[array].at[pl.ds(row + t * BLOCK, BLOCK), pl.ds(column, kv_width)],
                                kv.at[pl.ds(target, BLOCK), :],
                                sem_in,
                            )
                        )

                act() if condition is None else pl.when(condition)(act)

        def one_group(i, carry):
            block = i * together // spans
            owner = queries[0][3]
            for b in range(1, blocks):
                owner = jnp.where(block == b, queries[b][3], owner)
            within = i * together - block * spans

            def rows(u):
                return pl.ds(pl.multiple_of((i * together + u) * BLOCK, BLOCK), BLOCK)

            def load_q(u, g):
                return jnp.concatenate(
                    [q_all[rows(u), (g * GROUP + j) * HEAD_DIM : (g * GROUP + j + 1) * HEAD_DIM] for j in range(GROUP)],
                    axis=0,
                )

            def store_out(u, g, o):
                for j in range(GROUP):
                    o_all[rows(u), (g * GROUP + j) * HEAD_DIM : (g * GROUP + j + 1) * HEAD_DIM] = o[
                        j * BLOCK : (j + 1) * BLOCK
                    ]

            positions = [order[owner * spans + within + u] * BLOCK for u in range(together)]
            attend_spans(lengths, positions, heads, load_q, store_out, kv)
            for b in range(blocks):
                pl.when(block == b)(lambda b=b: out_copy(b, within).start())
            return carry

        def body():
            each_kv(lambda copy: copy.start())
            for b in range(blocks):
                q_copy(b).start()
            pltpu.make_async_copy(kv.at[pl.ds(0, total_rows), :], kv.at[pl.ds(0, total_rows), :], sem_in).wait()
            for b in range(blocks):
                q_copy(b).wait()
            lax.fori_loop(0, blocks * spans // together, one_group, 0)
            for b in range(blocks):
                for i in range(0, spans, together):
                    out_copy(b, i).wait()

        body() if active is None else pl.when(active(place))(body)

    smem = pl.BlockSpec(memory_space=pltpu.SMEM)
    hbm = pl.BlockSpec(memory_space=pl.ANY)
    pairs = int(100 * blocks * rows_here * heads * GROUP * 6 * COST[heads])
    shapes = [jax.ShapeDtypeStruct((rows_here, q_width), jnp.bfloat16)] * blocks
    if column is not None:
        shapes[-1] = jax.ShapeDtypeStruct((rows_here, HEADS * HEAD_DIM), jnp.bfloat16)
    given = [] if wide is None else [wide]
    return pl.pallas_call(
        kernel,
        out_shape=shapes,
        in_specs=[smem, smem] + [hbm] * (len(arrays) + len(given)),
        out_specs=[hbm] * blocks,
        scratch_shapes=[
            pltpu.VMEM((total_rows, kv_width), jnp.bfloat16),
            pltpu.VMEM((blocks * rows_here, q_width), jnp.bfloat16),
            pltpu.VMEM((blocks * rows_here, q_width), jnp.bfloat16),
            pltpu.SemaphoreType.DMA,
            pltpu.SemaphoreType.DMA,
        ],
        compiler_params=pltpu.CompilerParams(vmem_limit_bytes=VMEM_BYTES),
        cost_estimate=pl.CostEstimate(
            flops=pairs * 4 * HEAD_DIM, bytes_accessed=4 * blocks * rows_here * q_width, transcendentals=pairs
        ),
        input_output_aliases={2 + len(arrays): blocks - 1} if given else {},
        name=name,
    )(lengths, order, *arrays, *given)


def split(name, arrays, widths, plan, others=()):
    n, count = arrays[0].shape[0], len(widths)

    def kernel(*refs):
        inputs, outs = refs[: len(arrays)], refs[-2 - 2 * count : -2 - count]
        held, sems, sem_out = refs[-2 - count : -2], refs[-2], refs[-1]
        pair = lax.axis_index("seq") % 2

        def ins(o):
            to = 0
            for array, first, size in plan(pair)[o]:
                yield pltpu.make_async_copy(
                    inputs[array].at[:, pl.ds(first, size)], held[o].at[:, pl.ds(to, size)], sems.at[o]
                )
                to += size

        for o in range(count):
            for copy in ins(o):
                copy.start()
        for o in range(count):
            for copy in ins(o):
                copy.wait()
            pltpu.make_async_copy(held[o], outs[o], sem_out).start()
        for o in range(count):
            pltpu.make_async_copy(held[o], outs[o], sem_out).wait()

    hbm = pl.BlockSpec(memory_space=pl.ANY)
    return pl.pallas_call(
        kernel,
        out_shape=[jax.ShapeDtypeStruct((n, width), jnp.bfloat16) for width in widths],
        in_specs=[hbm] * (len(arrays) + len(others)),
        out_specs=[hbm] * count,
        scratch_shapes=[pltpu.VMEM((n, width), jnp.bfloat16) for width in widths]
        + [pltpu.SemaphoreType.DMA((count,)), pltpu.SemaphoreType.DMA],
        compiler_params=pltpu.CompilerParams(vmem_limit_bytes=VMEM_BYTES),
        cost_estimate=pl.CostEstimate(flops=0, bytes_accessed=4 * n * sum(widths), transcendentals=0),
        name=name,
    )(*arrays, *others)


def columns(array, first, size):
    return lax.dynamic_slice_in_dim(array, first, size, 1)


def kv_columns(keys, values, half, head, count):
    first, size = (half * KV_HALF + head) * HEAD_DIM, count * HEAD_DIM
    return [columns(keys, first, size), columns(values, first, size)]


def assemble(pair, mine, theirs):
    mine, theirs = jnp.concatenate(mine, axis=1), jnp.concatenate(theirs, axis=1)
    return jnp.where(
        pair == 0, jnp.concatenate([mine, theirs], axis=1), jnp.concatenate([theirs, mine], axis=1)
    )


def line_shards(queries, keys, values, lengths, order):
    devices = lax.axis_size("seq")
    line = devices // 2
    pair = lax.axis_index("seq") % 2
    rows_here = queries.shape[0]
    swap = [(i, i ^ 1) for i in range(devices)]

    def gather(shard):
        right, left = [], []
        r = l = shard
        for k in range(1, line):
            r = lax.ppermute(r, "seq", [(2 * z + x, 2 * z + 2 + x) for z in range(k - 1, line - 1) for x in range(2)])
            l = lax.ppermute(l, "seq", [(2 * z + x, 2 * z - 2 + x) for z in range(1, line + 1 - k) for x in range(2)])
            right.append(r)
            left.append(l)
        return [shard] + right + left

    mine, theirs = [], []
    heads = KV_HALF // 2
    for c in range(2):
        own = jnp.concatenate(kv_columns(keys, values, pair, c * heads, heads), axis=1)
        other = jnp.concatenate(kv_columns(keys, values, 1 - pair, c * heads, heads), axis=1)
        gathered = gather(jnp.concatenate([own, lax.ppermute(other, "seq", swap)], axis=0))
        q_other = lax.ppermute(
            columns(queries, (1 - pair) * KV_HALF * GQ + c * heads * GQ, heads * GQ), "seq", swap
        )

        def q_plan(place, pair, c=c):
            me = 2 * place + pair
            return [(0, 0, pair * KV_HALF * GQ + c * heads * GQ, me), (1, 0, 0, 2 * place + 1 - pair)]

        def kv_plan(place, pair):
            plan = []
            for half, x in enumerate((pair, 1 - pair)):
                row = half * rows_here
                plan.append((None, 2, row, 0, 2 * place + x))
                for k in range(1, line):
                    plan.append((place >= k, 2 + k, row, 0, 2 * (place - k) + x))
                    plan.append((place < k, 2 + line - 1 + line - k, row, 0, 2 * (place - k + line) + x))
            return plan

        a, b = attention("attention", heads, lengths, order, [queries, q_other] + gathered, q_plan, kv_plan)
        mine.append(a)
        theirs.append(lax.ppermute(b, "seq", swap))
    return assemble(pair, mine, theirs)


def hold(arrays, others=(), token=False):
    count = len(arrays)
    hbm = pl.BlockSpec(memory_space=pl.ANY)
    return pl.pallas_call(
        lambda *refs: None,
        out_shape=[jax.ShapeDtypeStruct(array.shape, array.dtype) for array in arrays]
        + [jax.ShapeDtypeStruct((16, 128), jnp.bfloat16)] * token,
        in_specs=[hbm] * (count + len(others)),
        out_specs=[hbm] * (count + token),
        input_output_aliases={i: i for i in range(count)},
        compiler_params=pltpu.CompilerParams(vmem_limit_bytes=WHOLE_VMEM),
        name="hold",
    )(*arrays, *others)


def short_shards(queries, keys, values, lengths, order):
    pair = lax.axis_index("seq") % 2
    n = queries.shape[0]
    parts = lax.axis_size("dp")
    both = ("dp", "seq")

    def permutation(links):
        return [(8 * d + 2 * a + x, 8 * d + 2 * b + x) for d in range(parts) for a, b in links for x in range(2)]

    across = [(8 * d + i, 8 * d + (i ^ 1)) for d in range(parts) for i in range(8)]
    outer = permutation([(z, z ^ 1) for z in range(4)])
    ends = permutation([(z, z ^ 3) for z in range(4)])

    def swap_x(a):
        return lax.ppermute(a, both, across)

    def swap_outer(a):
        return lax.ppermute(a, both, outer)

    def swap_ends(a):
        return lax.ppermute(a, both, ends)

    def rows(*blocks):
        return jnp.concatenate(blocks, axis=0)

    def near(place):
        return place + 1 - 2 * (place % 2)

    one, two = HEAD_DIM, 2 * HEAD_DIM
    kv_half, q_half = KV_HALF * HEAD_DIM, KV_HALF * GQ

    def kv_plan(pair):
        t = [[(a, half * kv_half, two) for a in range(2)] for half in (pair, 1 - pair)]
        w = [
            [(a, half * kv_half + head * one, one) for head in (2, 3) for a in range(2)] for half in (pair, 1 - pair)
        ]
        return t + w

    def q_plan(pair):
        return [[(0, (1 - pair) * q_half + i * 2 * GQ, 2 * GQ)] for i in range(2)]

    t_own, t_send, w_own, w_send = split("split_kv", [keys, values], [2 * two] * 4, kv_plan)
    t_par = swap_x(t_send)
    t_near_own, t_far_own = swap_outer(t_own), swap_ends(t_own)
    w_par = swap_x(w_send)
    t_near_par, t_far_par = swap_outer(t_par), swap_ends(t_par)
    t_out_own = swap_outer(t_far_own)
    qt_send, qw_send = split("split_q", [queries], [2 * GQ] * 2, q_plan, [w_par])
    qt_par, qw_par = swap_x(qt_send), swap_x(qw_send)
    t_out_par = swap_outer(t_far_par)
    (u_shard,) = hold([rows(w_own[:, :two], w_par[:, :two])], [t_far_par])
    v_shard = rows(w_own[:, two:], w_par[:, two:])
    u_far = swap_ends(u_shard)
    u_near, u_out = swap_outer(u_shard), swap_outer(u_far)
    v_far = swap_ends(v_shard)
    v_near, v_out = swap_outer(v_shard), swap_outer(v_far)

    def each_half(plan):
        def full(place, pair):
            return [
                (condition, array, row, column, 2 * owner + x)
                for half, x in enumerate((pair, 1 - pair))
                for condition, array, row, column, owner in plan(place, half)
            ]

        return full

    def t_queries(place, pair):
        return [(1, 0, 0, 2 * place + 1 - pair), (0, 0, pair * q_half, 2 * place + pair)]

    def t_keys(place, half):
        return [
            (None, 2 + half, 0, 0, place),
            (None, 4 + half, 0, 0, near(place)),
            (None, 6 + half, 0, 0, 3 - place),
            (None, 8 + half, 0, 0, 3 - near(place)),
        ]

    t_other, wide = attention(
        "attention_t",
        2,
        lengths,
        order,
        [queries, qt_par, t_own, t_par, t_near_own, t_near_par, t_far_own, t_far_par, t_out_own, t_out_par],
        t_queries,
        each_half(t_keys),
        column=lambda pair: pair * q_half,
    )
    t_theirs = swap_x(t_other)


    def w_queries(head):
        def own(place, pair):
            return [(0, 0, pair * q_half + head * GQ, 2 * place + pair)]

        def other(place, pair):
            return [(1, 0, (head - 2) * GQ, 2 * place + 1 - pair)]

        return own, other, lambda place, pair: other(place, pair) + own(place, pair)

    def w_keys(place, half):
        return [
            (None, 2, half * n, 0, place),
            (None, 3, half * n, 0, near(place)),
            (None, 4, half * n, 0, 3 - place),
            (None, 5, half * n, 0, 3 - near(place)),
        ]

    u_other, wide = attention(
        "attention_u",
        1,
        lengths,
        order,
        [queries, qw_par, u_shard, u_near, u_far, u_out],
        w_queries(2)[2],
        each_half(w_keys),
        wide=wide,
        column=lambda pair: pair * q_half + 2 * GQ,
    )
    u_theirs = swap_x(u_other)
    theirs = (1 - pair) * q_half
    wide = lax.dynamic_update_slice_in_dim(wide, t_theirs, theirs, 1)
    v_arrays = [queries, qw_par, v_shard, v_near, v_far, v_out]
    (v_other,) = attention(
        "attention_v_other", 1, lengths, order, v_arrays + [u_other], w_queries(3)[1], each_half(w_keys)
    )
    v_theirs = swap_x(v_other)
    (wide,) = attention(
        "attention_v_own",
        1,
        lengths,
        order,
        v_arrays + [v_other],
        w_queries(3)[0],
        each_half(w_keys),
        wide=wide,
        column=lambda pair: pair * q_half + 3 * GQ,
    )
    wide = lax.dynamic_update_slice_in_dim(wide, u_theirs, theirs + 2 * GQ, 1)
    return lax.dynamic_update_slice_in_dim(wide, v_theirs, theirs + 3 * GQ, 1)


def shards(queries, keys, values, lengths, order):
    whole = short_shards if lax.axis_size("seq") == 8 else line_shards
    return whole(queries, keys, values, lengths, order)


def solution(mesh):
    placed = (
        P(("dp", "seq"), None),
        P(("dp", "seq"), None),
        P(("dp", "seq"), None),
        P("dp"),
        P("dp"),
    )
    return jax.shard_map(
        shards, mesh=mesh, in_specs=placed, out_specs=P(("dp", "seq"), None), check_vma=False
    )
```

```python
import math
import jax
import jax.numpy as jnp
from jax import lax
from jax.experimental import pallas as pl
from jax.experimental.pallas import tpu as pltpu
from jax.sharding import PartitionSpec as P

HEADS = 32
KV_HEADS = 8
HEAD_DIM = 128
BLOCK = 64
DOC_MOST = 1024
GROUP = HEADS // KV_HEADS
KV_HALF = KV_HEADS // 2
KEY_STEP = 128
MOST_STEPS = -(-(DOC_MOST + BLOCK) // KEY_STEP)
EXP_SCALE = HEAD_DIM**-0.5 * math.log2(math.e)
GQ = GROUP * HEAD_DIM
COST = {1: 0.3, 2: 1}
VMEM_BYTES = 60 * 1024 * 1024
COUNTS = tuple(range(1, MOST_STEPS + 1))
TOGETHER = {1: 2, 2: 2}


def attend_spans(lengths, positions, heads, load_q, store_out, kv):
    spans = []
    most = jnp.int32(0)
    for row0 in positions:
        row = row0 + lax.broadcasted_iota(jnp.int32, (BLOCK, KEY_STEP), 0)
        low = jnp.int32(0)
        starts = jnp.zeros((BLOCK, KEY_STEP), jnp.int32)
        end = jnp.int32(0)
        for j in range(lengths.shape[0]):
            end = end + lengths[j]
            low = jnp.where(end <= row0, end, low)
            starts = jnp.where(end <= row, end, starts)
        spans.append((row0, row, starts))
        most = jnp.maximum(most, row0 + BLOCK - (low // BLOCK) * BLOCK)
    steps = (most + KEY_STEP - 1) // KEY_STEP

    def variant(count):
        width = count * KEY_STEP
        tiles = []
        for u, (row0, row, starts) in enumerate(spans):
            first = pl.multiple_of(jnp.maximum(row0 + BLOCK - width, 0), BLOCK)
            biases = []
            for t in range(count):
                col = first + t * KEY_STEP + lax.broadcasted_iota(jnp.int32, (BLOCK, KEY_STEP), 1)
                biases.append(jnp.where((col >= starts) & (col <= row), 0.0, -1e30).astype(jnp.float32))
            bias = jnp.concatenate(biases, axis=1)
            bias = jnp.concatenate([bias] * GROUP, axis=0)
            for g in range(heads):
                k = kv[pl.ds(first, width), g * HEAD_DIM : (g + 1) * HEAD_DIM]
                s = lax.dot_general(load_q(u, g), k, (((1,), (1,)), ((), ())), preferred_element_type=jnp.float32)
                tiles.append((u, g, first, s + bias))
        for u, g, first, s in tiles:
            v = kv[pl.ds(first, width), (heads + g) * HEAD_DIM : (heads + g + 1) * HEAD_DIM]
            top = jnp.max(s, axis=1, keepdims=True)
            p = jnp.exp2((s - top) * EXP_SCALE)
            total = jnp.sum(p, axis=1, keepdims=True)
            mixed = jnp.dot(p.astype(jnp.bfloat16), v, preferred_element_type=jnp.float32)
            store_out(u, g, (mixed / total).astype(jnp.bfloat16))

    def choose(counts):
        if len(counts) == 1:
            variant(counts[0])
            return
        half = len(counts) // 2
        small = steps <= counts[half - 1]
        pl.when(small)(lambda: choose(counts[:half]))
        pl.when(jnp.logical_not(small))(lambda: choose(counts[half:]))

    choose(COUNTS)


def attention(name, heads, lengths, order, arrays, q_plan, kv_plan, active=None, wide=None, column=None):
    total_rows = order.shape[0] * BLOCK
    rows_here = total_rows // lax.axis_size("seq")
    spans = rows_here // BLOCK
    q_width, kv_width = heads * GQ, 2 * heads * HEAD_DIM
    blocks = len(q_plan(0, 0))
    together = TOGETHER[heads]

    def kernel(lengths, order, *refs):
        inputs, outs = refs[: len(arrays)], refs[-5 - blocks : -5]
        kv, q_all, o_all, sem_in, sem_out = refs[-5:]
        me = lax.axis_index("seq")
        place = me // 2
        pair = me - 2 * place
        queries = q_plan(place, pair)

        def q_copy(b):
            array, row, column, _ = queries[b]
            return pltpu.make_async_copy(
                inputs[array].at[pl.ds(row, rows_here), pl.ds(column, q_width)],
                q_all.at[pl.ds(b * rows_here, rows_here), :],
                sem_in,
            )

        def out_copy(b, i):
            source = pl.multiple_of(b * rows_here + i * BLOCK, BLOCK)
            target = pl.multiple_of(i * BLOCK, BLOCK)
            size = together * BLOCK
            place = outs[b].at[pl.ds(target, size), :]
            if column is not None and b == blocks - 1:
                place = outs[b].at[pl.ds(target, size), pl.ds(column(pair), q_width)]
            return pltpu.make_async_copy(
                o_all.at[pl.ds(source, size), :], place, sem_out
            )

        def each_kv(action):
            for condition, array, row, column, owner in kv_plan(place, pair):

                def act(array=array, row=row, column=column, owner=owner):
                    for t in range(spans):
                        target = pl.multiple_of(order[owner * spans + t] * BLOCK, BLOCK)
                        action(
                            pltpu.make_async_copy(
                                inputs[array].at[pl.ds(row + t * BLOCK, BLOCK), pl.ds(column, kv_width)],
                                kv.at[pl.ds(target, BLOCK), :],
                                sem_in,
                            )
                        )

                act() if condition is None else pl.when(condition)(act)

        def one_group(i, carry):
            block = i * together // spans
            owner = queries[0][3]
            for b in range(1, blocks):
                owner = jnp.where(block == b, queries[b][3], owner)
            within = i * together - block * spans

            def rows(u):
                return pl.ds(pl.multiple_of((i * together + u) * BLOCK, BLOCK), BLOCK)

            def load_q(u, g):
                return jnp.concatenate(
                    [q_all[rows(u), (g * GROUP + j) * HEAD_DIM : (g * GROUP + j + 1) * HEAD_DIM] for j in range(GROUP)],
                    axis=0,
                )

            def store_out(u, g, o):
                for j in range(GROUP):
                    o_all[rows(u), (g * GROUP + j) * HEAD_DIM : (g * GROUP + j + 1) * HEAD_DIM] = o[
                        j * BLOCK : (j + 1) * BLOCK
                    ]

            positions = [order[owner * spans + within + u] * BLOCK for u in range(together)]
            attend_spans(lengths, positions, heads, load_q, store_out, kv)
            for b in range(blocks):
                pl.when(block == b)(lambda b=b: out_copy(b, within).start())
            return carry

        def body():
            each_kv(lambda copy: copy.start())
            for b in range(blocks):
                q_copy(b).start()
            pltpu.make_async_copy(kv.at[pl.ds(0, total_rows), :], kv.at[pl.ds(0, total_rows), :], sem_in).wait()
            for b in range(blocks):
                q_copy(b).wait()
            lax.fori_loop(0, blocks * spans // together, one_group, 0)
            for b in range(blocks):
                for i in range(0, spans, together):
                    out_copy(b, i).wait()

        body() if active is None else pl.when(active(place))(body)

    smem = pl.BlockSpec(memory_space=pltpu.SMEM)
    hbm = pl.BlockSpec(memory_space=pltpu.HBM)
    pairs = int(100 * blocks * rows_here * heads * GROUP * 6 * COST[heads])
    shapes = [jax.ShapeDtypeStruct((rows_here, q_width), jnp.bfloat16)] * blocks
    if column is not None:
        shapes[-1] = jax.ShapeDtypeStruct((rows_here, HEADS * HEAD_DIM), jnp.bfloat16)
    given = [] if wide is None else [wide]
    return pl.pallas_call(
        kernel,
        out_shape=shapes,
        in_specs=[smem, smem] + [hbm] * (len(arrays) + len(given)),
        out_specs=[hbm] * blocks,
        scratch_shapes=[
            pltpu.VMEM((total_rows, kv_width), jnp.bfloat16),
            pltpu.VMEM((blocks * rows_here, q_width), jnp.bfloat16),
            pltpu.VMEM((blocks * rows_here, q_width), jnp.bfloat16),
            pltpu.SemaphoreType.DMA,
            pltpu.SemaphoreType.DMA,
        ],
        compiler_params=pltpu.CompilerParams(vmem_limit_bytes=VMEM_BYTES),
        cost_estimate=pl.CostEstimate(
            flops=pairs * 4 * HEAD_DIM, bytes_accessed=4 * blocks * rows_here * q_width, transcendentals=pairs
        ),
        input_output_aliases={2 + len(arrays): blocks - 1} if given else {},
        name=name,
    )(lengths, order, *arrays, *given)


def split(name, arrays, widths, plan, others=()):
    n, count = arrays[0].shape[0], len(widths)

    def kernel(*refs):
        inputs, outs = refs[: len(arrays)], refs[-2 - 2 * count : -2 - count]
        held, sems, sem_out = refs[-2 - count : -2], refs[-2], refs[-1]
        pair = lax.axis_index("seq") % 2

        def ins(o):
            to = 0
            for array, first, size in plan(pair)[o]:
                yield pltpu.make_async_copy(
                    inputs[array].at[:, pl.ds(first, size)], held[o].at[:, pl.ds(to, size)], sems.at[o]
                )
                to += size

        for o in range(count):
            for copy in ins(o):
                copy.start()
        for o in range(count):
            for copy in ins(o):
                copy.wait()
            pltpu.make_async_copy(held[o], outs[o], sem_out).start()
        for o in range(count):
            pltpu.make_async_copy(held[o], outs[o], sem_out).wait()

    hbm = pl.BlockSpec(memory_space=pltpu.HBM)
    return pl.pallas_call(
        kernel,
        out_shape=[jax.ShapeDtypeStruct((n, width), jnp.bfloat16) for width in widths],
        in_specs=[hbm] * (len(arrays) + len(others)),
        out_specs=[hbm] * count,
        scratch_shapes=[pltpu.VMEM((n, width), jnp.bfloat16) for width in widths]
        + [pltpu.SemaphoreType.DMA((count,)), pltpu.SemaphoreType.DMA],
        compiler_params=pltpu.CompilerParams(vmem_limit_bytes=VMEM_BYTES),
        cost_estimate=pl.CostEstimate(flops=0, bytes_accessed=4 * n * sum(widths), transcendentals=0),
        name=name,
    )(*arrays, *others)


def columns(array, first, size):
    return lax.dynamic_slice_in_dim(array, first, size, 1)


def kv_columns(keys, values, half, head, count):
    first, size = (half * KV_HALF + head) * HEAD_DIM, count * HEAD_DIM
    return [columns(keys, first, size), columns(values, first, size)]


def assemble(pair, mine, theirs):
    mine, theirs = jnp.concatenate(mine, axis=1), jnp.concatenate(theirs, axis=1)
    return jnp.where(
        pair == 0, jnp.concatenate([mine, theirs], axis=1), jnp.concatenate([theirs, mine], axis=1)
    )


def line_shards(queries, keys, values, lengths, order):
    devices = lax.axis_size("seq")
    line = devices // 2
    pair = lax.axis_index("seq") % 2
    rows_here = queries.shape[0]
    swap = [(i, i ^ 1) for i in range(devices)]

    def gather(shard):
        right, left = [], []
        r = l = shard
        for k in range(1, line):
            r = lax.ppermute(r, "seq", [(2 * z + x, 2 * z + 2 + x) for z in range(k - 1, line - 1) for x in range(2)])
            l = lax.ppermute(l, "seq", [(2 * z + x, 2 * z - 2 + x) for z in range(1, line + 1 - k) for x in range(2)])
            right.append(r)
            left.append(l)
        return [shard] + right + left

    mine, theirs = [], []
    heads = KV_HALF // 2
    for c in range(2):
        own = jnp.concatenate(kv_columns(keys, values, pair, c * heads, heads), axis=1)
        other = jnp.concatenate(kv_columns(keys, values, 1 - pair, c * heads, heads), axis=1)
        gathered = gather(jnp.concatenate([own, lax.ppermute(other, "seq", swap)], axis=0))
        q_other = lax.ppermute(
            columns(queries, (1 - pair) * KV_HALF * GQ + c * heads * GQ, heads * GQ), "seq", swap
        )

        def q_plan(place, pair, c=c):
            me = 2 * place + pair
            return [(0, 0, pair * KV_HALF * GQ + c * heads * GQ, me), (1, 0, 0, 2 * place + 1 - pair)]

        def kv_plan(place, pair):
            plan = []
            for half, x in enumerate((pair, 1 - pair)):
                row = half * rows_here
                plan.append((None, 2, row, 0, 2 * place + x))
                for k in range(1, line):
                    plan.append((place >= k, 2 + k, row, 0, 2 * (place - k) + x))
                    plan.append((place < k, 2 + line - 1 + line - k, row, 0, 2 * (place - k + line) + x))
            return plan

        a, b = attention("attention", heads, lengths, order, [queries, q_other] + gathered, q_plan, kv_plan)
        mine.append(a)
        theirs.append(lax.ppermute(b, "seq", swap))
    return assemble(pair, mine, theirs)


def hold(arrays, others=(), token=False):
    count = len(arrays)
    hbm = pl.BlockSpec(memory_space=pltpu.HBM)
    return pl.pallas_call(
        lambda *refs: None,
        out_shape=[jax.ShapeDtypeStruct(array.shape, array.dtype) for array in arrays]
        + [jax.ShapeDtypeStruct((16, 128), jnp.bfloat16)] * token,
        in_specs=[hbm] * (count + len(others)),
        out_specs=[hbm] * (count + token),
        input_output_aliases={i: i for i in range(count)},
        compiler_params=pltpu.CompilerParams(vmem_limit_bytes=VMEM_BYTES),
        name="hold",
    )(*arrays, *others)


def short_shards(queries, keys, values, lengths, order):
    pair = lax.axis_index("seq") % 2
    n = queries.shape[0]
    parts = lax.axis_size("dp")
    both = ("dp", "seq")

    def permutation(links):
        return [(8 * d + 2 * a + x, 8 * d + 2 * b + x) for d in range(parts) for a, b in links for x in range(2)]

    across = [(8 * d + i, 8 * d + (i ^ 1)) for d in range(parts) for i in range(8)]
    outer = permutation([(z, z ^ 1) for z in range(4)])
    ends = permutation([(z, z ^ 3) for z in range(4)])

    def swap_x(a):
        return lax.ppermute(a, both, across)

    def swap_outer(a):
        return lax.ppermute(a, both, outer)

    def swap_ends(a):
        return lax.ppermute(a, both, ends)

    def rows(*blocks):
        return jnp.concatenate(blocks, axis=0)

    def near(place):
        return place + 1 - 2 * (place % 2)

    one, two = HEAD_DIM, 2 * HEAD_DIM
    kv_half, q_half = KV_HALF * HEAD_DIM, KV_HALF * GQ

    def kv_plan(pair):
        t = [[(a, half * kv_half, two) for a in range(2)] for half in (pair, 1 - pair)]
        w = [
            [(a, half * kv_half + head * one, one) for head in (2, 3) for a in range(2)] for half in (pair, 1 - pair)
        ]
        return t + w

    def q_plan(pair):
        return [[(0, (1 - pair) * q_half + i * 2 * GQ, 2 * GQ)] for i in range(2)]

    t_own, t_send, w_own, w_send = split("split_kv", [keys, values], [2 * two] * 4, kv_plan)
    t_par = swap_x(t_send)
    t_near_own, t_far_own = swap_outer(t_own), swap_ends(t_own)
    w_par = swap_x(w_send)
    t_near_par, t_far_par = swap_outer(t_par), swap_ends(t_par)
    t_out_own = swap_outer(t_far_own)
    qt_send, qw_send = split("split_q", [queries], [2 * GQ] * 2, q_plan, [w_par])
    qt_par, qw_par = swap_x(qt_send), swap_x(qw_send)
    t_out_par = swap_outer(t_far_par)
    (u_shard,) = hold([rows(w_own[:, :two], w_par[:, :two])], [t_far_par])
    v_shard = rows(w_own[:, two:], w_par[:, two:])
    u_far = swap_ends(u_shard)
    u_near, u_out = swap_outer(u_shard), swap_outer(u_far)
    v_far = swap_ends(v_shard)
    v_near, v_out = swap_outer(v_shard), swap_outer(v_far)

    def each_half(plan):
        def full(place, pair):
            return [
                (condition, array, row, column, 2 * owner + x)
                for half, x in enumerate((pair, 1 - pair))
                for condition, array, row, column, owner in plan(place, half)
            ]

        return full

    def t_queries(place, pair):
        return [(1, 0, 0, 2 * place + 1 - pair), (0, 0, pair * q_half, 2 * place + pair)]

    def t_keys(place, half):
        return [
            (None, 2 + half, 0, 0, place),
            (None, 4 + half, 0, 0, near(place)),
            (None, 6 + half, 0, 0, 3 - place),
            (None, 8 + half, 0, 0, 3 - near(place)),
        ]

    t_other, wide = attention(
        "attention_t",
        2,
        lengths,
        order,
        [queries, qt_par, t_own, t_par, t_near_own, t_near_par, t_far_own, t_far_par, t_out_own, t_out_par],
        t_queries,
        each_half(t_keys),
        column=lambda pair: pair * q_half,
    )
    t_theirs = swap_x(t_other)


    def w_queries(head):
        def own(place, pair):
            return [(0, 0, pair * q_half + head * GQ, 2 * place + pair)]

        def other(place, pair):
            return [(1, 0, (head - 2) * GQ, 2 * place + 1 - pair)]

        return own, other, lambda place, pair: other(place, pair) + own(place, pair)

    def w_keys(place, half):
        return [
            (None, 2, half * n, 0, place),
            (None, 3, half * n, 0, near(place)),
            (None, 4, half * n, 0, 3 - place),
            (None, 5, half * n, 0, 3 - near(place)),
        ]

    u_other, wide = attention(
        "attention_u",
        1,
        lengths,
        order,
        [queries, qw_par, u_shard, u_near, u_far, u_out],
        w_queries(2)[2],
        each_half(w_keys),
        wide=wide,
        column=lambda pair: pair * q_half + 2 * GQ,
    )
    u_theirs = swap_x(u_other)
    theirs = (1 - pair) * q_half
    wide = lax.dynamic_update_slice_in_dim(wide, t_theirs, theirs, 1)
    v_arrays = [queries, qw_par, v_shard, v_near, v_far, v_out]
    (v_other,) = attention(
        "attention_v_other", 1, lengths, order, v_arrays + [u_other], w_queries(3)[1], each_half(w_keys)
    )
    v_theirs = swap_x(v_other)
    (wide,) = attention(
        "attention_v_own",
        1,
        lengths,
        order,
        v_arrays + [v_other],
        w_queries(3)[0],
        each_half(w_keys),
        wide=wide,
        column=lambda pair: pair * q_half + 3 * GQ,
    )
    wide = lax.dynamic_update_slice_in_dim(wide, u_theirs, theirs + 2 * GQ, 1)
    return lax.dynamic_update_slice_in_dim(wide, v_theirs, theirs + 3 * GQ, 1)


def shards(queries, keys, values, lengths, order):
    whole = short_shards if lax.axis_size("seq") == 8 else line_shards
    return whole(queries, keys, values, lengths, order)


def solution(mesh):
    placed = (
        P(("dp", "seq"), None),
        P(("dp", "seq"), None),
        P(("dp", "seq"), None),
        P("dp"),
        P("dp"),
    )
    return jax.shard_map(
        shards, mesh=mesh, in_specs=placed, out_specs=P(("dp", "seq"), None), check_vma=False
    )
```

```python
import math
import jax
import jax.numpy as jnp
from jax import lax
from jax.experimental import pallas as pl
from jax.experimental.pallas import tpu as pltpu
from jax.sharding import PartitionSpec as P

HEADS = 32
KV_HEADS = 8
HEAD_DIM = 128
BLOCK = 64
DOC_MOST = 1024
GROUP = HEADS // KV_HEADS
KV_HALF = KV_HEADS // 2
KEY_STEP = 128
MOST_STEPS = -(-(DOC_MOST + BLOCK) // KEY_STEP)
EXP_SCALE = HEAD_DIM**-0.5 * math.log2(math.e)
GQ = GROUP * HEAD_DIM
COST = {1: 0.3, 2: 1}
VMEM_BYTES = 60 * 1024 * 1024
COUNTS = tuple(range(1, MOST_STEPS + 1))
TOGETHER = {1: 2, 2: 1}


def attend_spans(lengths, positions, heads, load_q, store_out, kv):
    spans = []
    most = jnp.int32(0)
    for row0 in positions:
        row = row0 + lax.broadcasted_iota(jnp.int32, (BLOCK, KEY_STEP), 0)
        low = jnp.int32(0)
        starts = jnp.zeros((BLOCK, KEY_STEP), jnp.int32)
        end = jnp.int32(0)
        for j in range(lengths.shape[0]):
            end = end + lengths[j]
            low = jnp.where(end <= row0, end, low)
            starts = jnp.where(end <= row, end, starts)
        spans.append((row0, row, starts))
        most = jnp.maximum(most, row0 + BLOCK - (low // BLOCK) * BLOCK)
    steps = (most + KEY_STEP - 1) // KEY_STEP

    def variant(count):
        width = count * KEY_STEP
        tiles = []
        for u, (row0, row, starts) in enumerate(spans):
            first = pl.multiple_of(jnp.maximum(row0 + BLOCK - width, 0), BLOCK)
            biases = []
            for t in range(count):
                col = first + t * KEY_STEP + lax.broadcasted_iota(jnp.int32, (BLOCK, KEY_STEP), 1)
                biases.append(jnp.where((col >= starts) & (col <= row), 0.0, -1e30).astype(jnp.float32))
            bias = jnp.concatenate(biases, axis=1)
            bias = jnp.concatenate([bias] * GROUP, axis=0)
            for g in range(heads):
                k = kv[pl.ds(first, width), g * HEAD_DIM : (g + 1) * HEAD_DIM]
                s = lax.dot_general(load_q(u, g), k, (((1,), (1,)), ((), ())), preferred_element_type=jnp.float32)
                tiles.append((u, g, first, s + bias))
        for u, g, first, s in tiles:
            v = kv[pl.ds(first, width), (heads + g) * HEAD_DIM : (heads + g + 1) * HEAD_DIM]
            top = jnp.max(s, axis=1, keepdims=True)
            p = jnp.exp2((s - top) * EXP_SCALE)
            total = jnp.sum(p, axis=1, keepdims=True)
            mixed = jnp.dot(p.astype(jnp.bfloat16), v, preferred_element_type=jnp.float32)
            store_out(u, g, (mixed / total).astype(jnp.bfloat16))

    def choose(counts):
        if len(counts) == 1:
            variant(counts[0])
            return
        half = len(counts) // 2
        small = steps <= counts[half - 1]
        pl.when(small)(lambda: choose(counts[:half]))
        pl.when(jnp.logical_not(small))(lambda: choose(counts[half:]))

    choose(COUNTS)


def attention(name, heads, lengths, order, arrays, q_plan, kv_plan, active=None, wide=None, column=None):
    total_rows = order.shape[0] * BLOCK
    rows_here = total_rows // lax.axis_size("seq")
    spans = rows_here // BLOCK
    q_width, kv_width = heads * GQ, 2 * heads * HEAD_DIM
    blocks = len(q_plan(0, 0))
    together = TOGETHER[heads]

    def kernel(lengths, order, *refs):
        inputs, outs = refs[: len(arrays)], refs[-5 - blocks : -5]
        kv, q_all, o_all, sem_in, sem_out = refs[-5:]
        me = lax.axis_index("seq")
        place = me // 2
        pair = me - 2 * place
        queries = q_plan(place, pair)

        def q_copy(b):
            array, row, column, _ = queries[b]
            return pltpu.make_async_copy(
                inputs[array].at[pl.ds(row, rows_here), pl.ds(column, q_width)],
                q_all.at[pl.ds(b * rows_here, rows_here), :],
                sem_in,
            )

        def out_copy(b, i):
            source = pl.multiple_of(b * rows_here + i * BLOCK, BLOCK)
            target = pl.multiple_of(i * BLOCK, BLOCK)
            size = together * BLOCK
            place = outs[b].at[pl.ds(target, size), :]
            if column is not None and b == blocks - 1:
                place = outs[b].at[pl.ds(target, size), pl.ds(column(pair), q_width)]
            return pltpu.make_async_copy(
                o_all.at[pl.ds(source, size), :], place, sem_out
            )

        def each_kv(action):
            for condition, array, row, column, owner in kv_plan(place, pair):

                def act(array=array, row=row, column=column, owner=owner):
                    for t in range(spans):
                        target = pl.multiple_of(order[owner * spans + t] * BLOCK, BLOCK)
                        action(
                            pltpu.make_async_copy(
                                inputs[array].at[pl.ds(row + t * BLOCK, BLOCK), pl.ds(column, kv_width)],
                                kv.at[pl.ds(target, BLOCK), :],
                                sem_in,
                            )
                        )

                act() if condition is None else pl.when(condition)(act)

        def one_group(i, carry):
            block = i * together // spans
            owner = queries[0][3]
            for b in range(1, blocks):
                owner = jnp.where(block == b, queries[b][3], owner)
            within = i * together - block * spans

            def rows(u):
                return pl.ds(pl.multiple_of((i * together + u) * BLOCK, BLOCK), BLOCK)

            def load_q(u, g):
                return jnp.concatenate(
                    [q_all[rows(u), (g * GROUP + j) * HEAD_DIM : (g * GROUP + j + 1) * HEAD_DIM] for j in range(GROUP)],
                    axis=0,
                )

            def store_out(u, g, o):
                for j in range(GROUP):
                    o_all[rows(u), (g * GROUP + j) * HEAD_DIM : (g * GROUP + j + 1) * HEAD_DIM] = o[
                        j * BLOCK : (j + 1) * BLOCK
                    ]

            positions = [order[owner * spans + within + u] * BLOCK for u in range(together)]
            attend_spans(lengths, positions, heads, load_q, store_out, kv)
            for b in range(blocks):
                pl.when(block == b)(lambda b=b: out_copy(b, within).start())
            return carry

        def body():
            each_kv(lambda copy: copy.start())
            for b in range(blocks):
                q_copy(b).start()
            pltpu.make_async_copy(kv.at[pl.ds(0, total_rows), :], kv.at[pl.ds(0, total_rows), :], sem_in).wait()
            for b in range(blocks):
                q_copy(b).wait()
            lax.fori_loop(0, blocks * spans // together, one_group, 0)
            for b in range(blocks):
                for i in range(0, spans, together):
                    out_copy(b, i).wait()

        body() if active is None else pl.when(active(place))(body)

    smem = pl.BlockSpec(memory_space=pltpu.SMEM)
    hbm = pl.BlockSpec(memory_space=pltpu.HBM)
    pairs = int(100 * blocks * rows_here * heads * GROUP * 6 * COST[heads])
    shapes = [jax.ShapeDtypeStruct((rows_here, q_width), jnp.bfloat16)] * blocks
    if column is not None:
        shapes[-1] = jax.ShapeDtypeStruct((rows_here, HEADS * HEAD_DIM), jnp.bfloat16)
    given = [] if wide is None else [wide]
    return pl.pallas_call(
        kernel,
        out_shape=shapes,
        in_specs=[smem, smem] + [hbm] * (len(arrays) + len(given)),
        out_specs=[hbm] * blocks,
        scratch_shapes=[
            pltpu.VMEM((total_rows, kv_width), jnp.bfloat16),
            pltpu.VMEM((blocks * rows_here, q_width), jnp.bfloat16),
            pltpu.VMEM((blocks * rows_here, q_width), jnp.bfloat16),
            pltpu.SemaphoreType.DMA,
            pltpu.SemaphoreType.DMA,
        ],
        compiler_params=pltpu.CompilerParams(vmem_limit_bytes=VMEM_BYTES),
        cost_estimate=pl.CostEstimate(
            flops=pairs * 4 * HEAD_DIM, bytes_accessed=4 * blocks * rows_here * q_width, transcendentals=pairs
        ),
        input_output_aliases={2 + len(arrays): blocks - 1} if given else {},
        name=name,
    )(lengths, order, *arrays, *given)


def split(name, arrays, widths, plan, others=()):
    n, count = arrays[0].shape[0], len(widths)

    def kernel(*refs):
        inputs, outs = refs[: len(arrays)], refs[-2 - 2 * count : -2 - count]
        held, sems, sem_out = refs[-2 - count : -2], refs[-2], refs[-1]
        pair = lax.axis_index("seq") % 2

        def ins(o):
            to = 0
            for array, first, size in plan(pair)[o]:
                yield pltpu.make_async_copy(
                    inputs[array].at[:, pl.ds(first, size)], held[o].at[:, pl.ds(to, size)], sems.at[o]
                )
                to += size

        for o in range(count):
            for copy in ins(o):
                copy.start()
        for o in range(count):
            for copy in ins(o):
                copy.wait()
            pltpu.make_async_copy(held[o], outs[o], sem_out).start()
        for o in range(count):
            pltpu.make_async_copy(held[o], outs[o], sem_out).wait()

    hbm = pl.BlockSpec(memory_space=pltpu.HBM)
    return pl.pallas_call(
        kernel,
        out_shape=[jax.ShapeDtypeStruct((n, width), jnp.bfloat16) for width in widths],
        in_specs=[hbm] * (len(arrays) + len(others)),
        out_specs=[hbm] * count,
        scratch_shapes=[pltpu.VMEM((n, width), jnp.bfloat16) for width in widths]
        + [pltpu.SemaphoreType.DMA((count,)), pltpu.SemaphoreType.DMA],
        compiler_params=pltpu.CompilerParams(vmem_limit_bytes=VMEM_BYTES),
        cost_estimate=pl.CostEstimate(flops=0, bytes_accessed=4 * n * sum(widths), transcendentals=0),
        name=name,
    )(*arrays, *others)


def columns(array, first, size):
    return lax.dynamic_slice_in_dim(array, first, size, 1)


def kv_columns(keys, values, half, head, count):
    first, size = (half * KV_HALF + head) * HEAD_DIM, count * HEAD_DIM
    return [columns(keys, first, size), columns(values, first, size)]


def assemble(pair, mine, theirs):
    mine, theirs = jnp.concatenate(mine, axis=1), jnp.concatenate(theirs, axis=1)
    return jnp.where(
        pair == 0, jnp.concatenate([mine, theirs], axis=1), jnp.concatenate([theirs, mine], axis=1)
    )


def line_shards(queries, keys, values, lengths, order):
    devices = lax.axis_size("seq")
    line = devices // 2
    pair = lax.axis_index("seq") % 2
    rows_here = queries.shape[0]
    swap = [(i, i ^ 1) for i in range(devices)]

    def gather(shard):
        right, left = [], []
        r = l = shard
        for k in range(1, line):
            r = lax.ppermute(r, "seq", [(2 * z + x, 2 * z + 2 + x) for z in range(k - 1, line - 1) for x in range(2)])
            l = lax.ppermute(l, "seq", [(2 * z + x, 2 * z - 2 + x) for z in range(1, line + 1 - k) for x in range(2)])
            right.append(r)
            left.append(l)
        return [shard] + right + left

    mine, theirs = [], []
    heads = KV_HALF // 2
    for c in range(2):
        own = jnp.concatenate(kv_columns(keys, values, pair, c * heads, heads), axis=1)
        other = jnp.concatenate(kv_columns(keys, values, 1 - pair, c * heads, heads), axis=1)
        gathered = gather(jnp.concatenate([own, lax.ppermute(other, "seq", swap)], axis=0))
        q_other = lax.ppermute(
            columns(queries, (1 - pair) * KV_HALF * GQ + c * heads * GQ, heads * GQ), "seq", swap
        )

        def q_plan(place, pair, c=c):
            me = 2 * place + pair
            return [(0, 0, pair * KV_HALF * GQ + c * heads * GQ, me), (1, 0, 0, 2 * place + 1 - pair)]

        def kv_plan(place, pair):
            plan = []
            for half, x in enumerate((pair, 1 - pair)):
                row = half * rows_here
                plan.append((None, 2, row, 0, 2 * place + x))
                for k in range(1, line):
                    plan.append((place >= k, 2 + k, row, 0, 2 * (place - k) + x))
                    plan.append((place < k, 2 + line - 1 + line - k, row, 0, 2 * (place - k + line) + x))
            return plan

        a, b = attention("attention", heads, lengths, order, [queries, q_other] + gathered, q_plan, kv_plan)
        mine.append(a)
        theirs.append(lax.ppermute(b, "seq", swap))
    return assemble(pair, mine, theirs)


def hold(arrays, others=(), token=False):
    count = len(arrays)
    hbm = pl.BlockSpec(memory_space=pltpu.HBM)
    return pl.pallas_call(
        lambda *refs: None,
        out_shape=[jax.ShapeDtypeStruct(array.shape, array.dtype) for array in arrays]
        + [jax.ShapeDtypeStruct((16, 128), jnp.bfloat16)] * token,
        in_specs=[hbm] * (count + len(others)),
        out_specs=[hbm] * (count + token),
        input_output_aliases={i: i for i in range(count)},
        compiler_params=pltpu.CompilerParams(vmem_limit_bytes=VMEM_BYTES),
        name="hold",
    )(*arrays, *others)


def short_shards(queries, keys, values, lengths, order):
    pair = lax.axis_index("seq") % 2
    n = queries.shape[0]
    parts = lax.axis_size("dp")
    both = ("dp", "seq")

    def permutation(links):
        return [(8 * d + 2 * a + x, 8 * d + 2 * b + x) for d in range(parts) for a, b in links for x in range(2)]

    across = [(8 * d + i, 8 * d + (i ^ 1)) for d in range(parts) for i in range(8)]
    outer = permutation([(z, z ^ 1) for z in range(4)])
    ends = permutation([(z, z ^ 3) for z in range(4)])

    def swap_x(a):
        return lax.ppermute(a, both, across)

    def swap_outer(a):
        return lax.ppermute(a, both, outer)

    def swap_ends(a):
        return lax.ppermute(a, both, ends)

    def rows(*blocks):
        return jnp.concatenate(blocks, axis=0)

    def near(place):
        return place + 1 - 2 * (place % 2)

    one, two = HEAD_DIM, 2 * HEAD_DIM
    kv_half, q_half = KV_HALF * HEAD_DIM, KV_HALF * GQ

    def kv_plan(pair):
        t = [[(a, half * kv_half, two) for a in range(2)] for half in (pair, 1 - pair)]
        w = [
            [(a, half * kv_half + head * one, one) for head in (2, 3) for a in range(2)] for half in (pair, 1 - pair)
        ]
        return t + w

    def q_plan(pair):
        return [[(0, (1 - pair) * q_half + i * 2 * GQ, 2 * GQ)] for i in range(2)]

    t_own, t_send, w_own, w_send = split("split_kv", [keys, values], [2 * two] * 4, kv_plan)
    t_par = swap_x(t_send)
    t_near_own, t_far_own = swap_outer(t_own), swap_ends(t_own)
    w_par = swap_x(w_send)
    t_near_par, t_far_par = swap_outer(t_par), swap_ends(t_par)
    t_out_own = swap_outer(t_far_own)
    qt_send, qw_send = split("split_q", [queries], [2 * GQ] * 2, q_plan, [w_par])
    qt_par, qw_par = swap_x(qt_send), swap_x(qw_send)
    t_out_par = swap_outer(t_far_par)
    (u_shard,) = hold([rows(w_own[:, :two], w_par[:, :two])], [t_far_par])
    v_shard = rows(w_own[:, two:], w_par[:, two:])
    u_far = swap_ends(u_shard)
    u_near, u_out = swap_outer(u_shard), swap_outer(u_far)
    v_far = swap_ends(v_shard)
    v_near, v_out = swap_outer(v_shard), swap_outer(v_far)

    def each_half(plan):
        def full(place, pair):
            return [
                (condition, array, row, column, 2 * owner + x)
                for half, x in enumerate((pair, 1 - pair))
                for condition, array, row, column, owner in plan(place, half)
            ]

        return full

    def t_queries(place, pair):
        return [(1, 0, 0, 2 * place + 1 - pair), (0, 0, pair * q_half, 2 * place + pair)]

    def t_keys(place, half):
        return [
            (None, 2 + half, 0, 0, place),
            (None, 4 + half, 0, 0, near(place)),
            (None, 6 + half, 0, 0, 3 - place),
            (None, 8 + half, 0, 0, 3 - near(place)),
        ]

    t_other, wide = attention(
        "attention_t",
        2,
        lengths,
        order,
        [queries, qt_par, t_own, t_par, t_near_own, t_near_par, t_far_own, t_far_par, t_out_own, t_out_par],
        t_queries,
        each_half(t_keys),
        column=lambda pair: pair * q_half,
    )
    t_theirs = swap_x(t_other)


    def w_queries(head):
        def own(place, pair):
            return [(0, 0, pair * q_half + head * GQ, 2 * place + pair)]

        def other(place, pair):
            return [(1, 0, (head - 2) * GQ, 2 * place + 1 - pair)]

        return own, other, lambda place, pair: other(place, pair) + own(place, pair)

    def w_keys(place, half):
        return [
            (None, 2, half * n, 0, place),
            (None, 3, half * n, 0, near(place)),
            (None, 4, half * n, 0, 3 - place),
            (None, 5, half * n, 0, 3 - near(place)),
        ]

    u_other, wide = attention(
        "attention_u",
        1,
        lengths,
        order,
        [queries, qw_par, u_shard, u_near, u_far, u_out],
        w_queries(2)[2],
        each_half(w_keys),
        wide=wide,
        column=lambda pair: pair * q_half + 2 * GQ,
    )
    u_theirs = swap_x(u_other)
    theirs = (1 - pair) * q_half
    wide = lax.dynamic_update_slice_in_dim(wide, t_theirs, theirs, 1)
    v_arrays = [queries, qw_par, v_shard, v_near, v_far, v_out]
    (v_other,) = attention(
        "attention_v_other", 1, lengths, order, v_arrays + [u_other], w_queries(3)[1], each_half(w_keys)
    )
    v_theirs = swap_x(v_other)
    (wide,) = attention(
        "attention_v_own",
        1,
        lengths,
        order,
        v_arrays + [v_other],
        w_queries(3)[0],
        each_half(w_keys),
        wide=wide,
        column=lambda pair: pair * q_half + 3 * GQ,
    )
    wide = lax.dynamic_update_slice_in_dim(wide, u_theirs, theirs + 2 * GQ, 1)
    return lax.dynamic_update_slice_in_dim(wide, v_theirs, theirs + 3 * GQ, 1)


def shards(queries, keys, values, lengths, order):
    whole = short_shards if lax.axis_size("seq") == 8 else line_shards
    return whole(queries, keys, values, lengths, order)


def solution(mesh):
    placed = (
        P(("dp", "seq"), None),
        P(("dp", "seq"), None),
        P(("dp", "seq"), None),
        P("dp"),
        P("dp"),
    )
    return jax.shard_map(
        shards, mesh=mesh, in_specs=placed, out_specs=P(("dp", "seq"), None), check_vma=False
    )
```

```python
import math
import jax
import jax.numpy as jnp
from jax import lax
from jax.experimental import pallas as pl
from jax.experimental.pallas import tpu as pltpu
from jax.sharding import PartitionSpec as P

HEADS = 32
KV_HEADS = 8
HEAD_DIM = 128
BLOCK = 64
DOC_MOST = 1024
GROUP = HEADS // KV_HEADS
KV_HALF = KV_HEADS // 2
KEY_STEP = 128
MOST_STEPS = -(-(DOC_MOST + BLOCK) // KEY_STEP)
EXP_SCALE = HEAD_DIM**-0.5 * math.log2(math.e)
GQ = GROUP * HEAD_DIM
COST = {1: 0.3, 2: 1}
VMEM_BYTES = 60 * 1024 * 1024
COUNTS = tuple(range(1, MOST_STEPS + 1))
TOGETHER = {1: 2, 2: 1}


def attend_spans(lengths, positions, heads, load_q, store_out, kv):
    spans = []
    most = jnp.int32(0)
    for row0 in positions:
        row = row0 + lax.broadcasted_iota(jnp.int32, (BLOCK, KEY_STEP), 0)
        low = jnp.int32(0)
        starts = jnp.zeros((BLOCK, KEY_STEP), jnp.int32)
        end = jnp.int32(0)
        for j in range(lengths.shape[0]):
            end = end + lengths[j]
            low = jnp.where(end <= row0, end, low)
            starts = jnp.where(end <= row, end, starts)
        spans.append((row0, row, starts))
        most = jnp.maximum(most, row0 + BLOCK - (low // BLOCK) * BLOCK)
    steps = (most + KEY_STEP - 1) // KEY_STEP

    def variant(count):
        width = count * KEY_STEP
        tiles = []
        for u, (row0, row, starts) in enumerate(spans):
            first = pl.multiple_of(jnp.maximum(row0 + BLOCK - width, 0), BLOCK)
            biases = []
            for t in range(count):
                col = first + t * KEY_STEP + lax.broadcasted_iota(jnp.int32, (BLOCK, KEY_STEP), 1)
                biases.append(jnp.where((col >= starts) & (col <= row), 0.0, -1e30).astype(jnp.float32))
            bias = jnp.concatenate(biases, axis=1)
            bias = jnp.concatenate([bias] * GROUP, axis=0)
            for g in range(heads):
                k = kv[pl.ds(first, width), g * HEAD_DIM : (g + 1) * HEAD_DIM]
                s = lax.dot_general(load_q(u, g), k, (((1,), (1,)), ((), ())), preferred_element_type=jnp.float32)
                tiles.append((u, g, first, s + bias))
        for u, g, first, s in tiles:
            v = kv[pl.ds(first, width), (heads + g) * HEAD_DIM : (heads + g + 1) * HEAD_DIM]
            top = jnp.max(s, axis=1, keepdims=True)
            p = jnp.exp2((s - top) * EXP_SCALE)
            total = jnp.sum(p, axis=1, keepdims=True)
            mixed = jnp.dot(p.astype(jnp.bfloat16), v, preferred_element_type=jnp.float32)
            store_out(u, g, (mixed * (1.0 / total)).astype(jnp.bfloat16))

    def choose(counts):
        if len(counts) == 1:
            variant(counts[0])
            return
        half = len(counts) // 2
        small = steps <= counts[half - 1]
        pl.when(small)(lambda: choose(counts[:half]))
        pl.when(jnp.logical_not(small))(lambda: choose(counts[half:]))

    choose(COUNTS)


def attention(name, heads, lengths, order, arrays, q_plan, kv_plan, active=None, wide=None, column=None):
    total_rows = order.shape[0] * BLOCK
    rows_here = total_rows // lax.axis_size("seq")
    spans = rows_here // BLOCK
    q_width, kv_width = heads * GQ, 2 * heads * HEAD_DIM
    blocks = len(q_plan(0, 0))
    together = TOGETHER[heads]

    def kernel(lengths, order, *refs):
        inputs, outs = refs[: len(arrays)], refs[-5 - blocks : -5]
        kv, q_all, o_all, sem_in, sem_out = refs[-5:]
        me = lax.axis_index("seq")
        place = me // 2
        pair = me - 2 * place
        queries = q_plan(place, pair)

        def q_copy(b):
            array, row, column, _ = queries[b]
            return pltpu.make_async_copy(
                inputs[array].at[pl.ds(row, rows_here), pl.ds(column, q_width)],
                q_all.at[pl.ds(b * rows_here, rows_here), :],
                sem_in,
            )

        def out_copy(b, i):
            source = pl.multiple_of(b * rows_here + i * BLOCK, BLOCK)
            target = pl.multiple_of(i * BLOCK, BLOCK)
            size = together * BLOCK
            place = outs[b].at[pl.ds(target, size), :]
            if column is not None and b == blocks - 1:
                place = outs[b].at[pl.ds(target, size), pl.ds(column(pair), q_width)]
            return pltpu.make_async_copy(
                o_all.at[pl.ds(source, size), :], place, sem_out
            )

        def each_kv(action):
            for condition, array, row, column, owner in kv_plan(place, pair):

                def act(array=array, row=row, column=column, owner=owner):
                    for t in range(spans):
                        target = pl.multiple_of(order[owner * spans + t] * BLOCK, BLOCK)
                        action(
                            pltpu.make_async_copy(
                                inputs[array].at[pl.ds(row + t * BLOCK, BLOCK), pl.ds(column, kv_width)],
                                kv.at[pl.ds(target, BLOCK), :],
                                sem_in,
                            )
                        )

                act() if condition is None else pl.when(condition)(act)

        def one_group(i, carry):
            block = i * together // spans
            owner = queries[0][3]
            for b in range(1, blocks):
                owner = jnp.where(block == b, queries[b][3], owner)
            within = i * together - block * spans

            def rows(u):
                return pl.ds(pl.multiple_of((i * together + u) * BLOCK, BLOCK), BLOCK)

            def load_q(u, g):
                return jnp.concatenate(
                    [q_all[rows(u), (g * GROUP + j) * HEAD_DIM : (g * GROUP + j + 1) * HEAD_DIM] for j in range(GROUP)],
                    axis=0,
                )

            def store_out(u, g, o):
                for j in range(GROUP):
                    o_all[rows(u), (g * GROUP + j) * HEAD_DIM : (g * GROUP + j + 1) * HEAD_DIM] = o[
                        j * BLOCK : (j + 1) * BLOCK
                    ]

            positions = [order[owner * spans + within + u] * BLOCK for u in range(together)]
            attend_spans(lengths, positions, heads, load_q, store_out, kv)
            for b in range(blocks):
                pl.when(block == b)(lambda b=b: out_copy(b, within).start())
            return carry

        def body():
            each_kv(lambda copy: copy.start())
            for b in range(blocks):
                q_copy(b).start()
            pltpu.make_async_copy(kv.at[pl.ds(0, total_rows), :], kv.at[pl.ds(0, total_rows), :], sem_in).wait()
            for b in range(blocks):
                q_copy(b).wait()
            lax.fori_loop(0, blocks * spans // together, one_group, 0)
            for b in range(blocks):
                for i in range(0, spans, together):
                    out_copy(b, i).wait()

        body() if active is None else pl.when(active(place))(body)

    smem = pl.BlockSpec(memory_space=pltpu.SMEM)
    hbm = pl.BlockSpec(memory_space=pltpu.HBM)
    pairs = int(100 * blocks * rows_here * heads * GROUP * 6 * COST[heads])
    shapes = [jax.ShapeDtypeStruct((rows_here, q_width), jnp.bfloat16)] * blocks
    if column is not None:
        shapes[-1] = jax.ShapeDtypeStruct((rows_here, HEADS * HEAD_DIM), jnp.bfloat16)
    given = [] if wide is None else [wide]
    return pl.pallas_call(
        kernel,
        out_shape=shapes,
        in_specs=[smem, smem] + [hbm] * (len(arrays) + len(given)),
        out_specs=[hbm] * blocks,
        scratch_shapes=[
            pltpu.VMEM((total_rows, kv_width), jnp.bfloat16),
            pltpu.VMEM((blocks * rows_here, q_width), jnp.bfloat16),
            pltpu.VMEM((blocks * rows_here, q_width), jnp.bfloat16),
            pltpu.SemaphoreType.DMA,
            pltpu.SemaphoreType.DMA,
        ],
        compiler_params=pltpu.CompilerParams(vmem_limit_bytes=VMEM_BYTES),
        cost_estimate=pl.CostEstimate(
            flops=pairs * 4 * HEAD_DIM, bytes_accessed=4 * blocks * rows_here * q_width, transcendentals=pairs
        ),
        input_output_aliases={2 + len(arrays): blocks - 1} if given else {},
        name=name,
    )(lengths, order, *arrays, *given)


def split(name, arrays, widths, plan, others=()):
    n, count = arrays[0].shape[0], len(widths)

    def kernel(*refs):
        inputs, outs = refs[: len(arrays)], refs[-2 - 2 * count : -2 - count]
        held, sems, sem_out = refs[-2 - count : -2], refs[-2], refs[-1]
        pair = lax.axis_index("seq") % 2

        def ins(o):
            to = 0
            for array, first, size in plan(pair)[o]:
                yield pltpu.make_async_copy(
                    inputs[array].at[:, pl.ds(first, size)], held[o].at[:, pl.ds(to, size)], sems.at[o]
                )
                to += size

        for o in range(count):
            for copy in ins(o):
                copy.start()
        for o in range(count):
            for copy in ins(o):
                copy.wait()
            pltpu.make_async_copy(held[o], outs[o], sem_out).start()
        for o in range(count):
            pltpu.make_async_copy(held[o], outs[o], sem_out).wait()

    hbm = pl.BlockSpec(memory_space=pltpu.HBM)
    return pl.pallas_call(
        kernel,
        out_shape=[jax.ShapeDtypeStruct((n, width), jnp.bfloat16) for width in widths],
        in_specs=[hbm] * (len(arrays) + len(others)),
        out_specs=[hbm] * count,
        scratch_shapes=[pltpu.VMEM((n, width), jnp.bfloat16) for width in widths]
        + [pltpu.SemaphoreType.DMA((count,)), pltpu.SemaphoreType.DMA],
        compiler_params=pltpu.CompilerParams(vmem_limit_bytes=VMEM_BYTES),
        cost_estimate=pl.CostEstimate(flops=0, bytes_accessed=4 * n * sum(widths), transcendentals=0),
        name=name,
    )(*arrays, *others)


def columns(array, first, size):
    return lax.dynamic_slice_in_dim(array, first, size, 1)


def kv_columns(keys, values, half, head, count):
    first, size = (half * KV_HALF + head) * HEAD_DIM, count * HEAD_DIM
    return [columns(keys, first, size), columns(values, first, size)]


def assemble(pair, mine, theirs):
    mine, theirs = jnp.concatenate(mine, axis=1), jnp.concatenate(theirs, axis=1)
    return jnp.where(
        pair == 0, jnp.concatenate([mine, theirs], axis=1), jnp.concatenate([theirs, mine], axis=1)
    )


def line_shards(queries, keys, values, lengths, order):
    devices = lax.axis_size("seq")
    line = devices // 2
    pair = lax.axis_index("seq") % 2
    rows_here = queries.shape[0]
    swap = [(i, i ^ 1) for i in range(devices)]

    def gather(shard):
        right, left = [], []
        r = l = shard
        for k in range(1, line):
            r = lax.ppermute(r, "seq", [(2 * z + x, 2 * z + 2 + x) for z in range(k - 1, line - 1) for x in range(2)])
            l = lax.ppermute(l, "seq", [(2 * z + x, 2 * z - 2 + x) for z in range(1, line + 1 - k) for x in range(2)])
            right.append(r)
            left.append(l)
        return [shard] + right + left

    mine, theirs = [], []
    heads = KV_HALF // 2
    for c in range(2):
        own = jnp.concatenate(kv_columns(keys, values, pair, c * heads, heads), axis=1)
        other = jnp.concatenate(kv_columns(keys, values, 1 - pair, c * heads, heads), axis=1)
        gathered = gather(jnp.concatenate([own, lax.ppermute(other, "seq", swap)], axis=0))
        q_other = lax.ppermute(
            columns(queries, (1 - pair) * KV_HALF * GQ + c * heads * GQ, heads * GQ), "seq", swap
        )

        def q_plan(place, pair, c=c):
            me = 2 * place + pair
            return [(0, 0, pair * KV_HALF * GQ + c * heads * GQ, me), (1, 0, 0, 2 * place + 1 - pair)]

        def kv_plan(place, pair):
            plan = []
            for half, x in enumerate((pair, 1 - pair)):
                row = half * rows_here
                plan.append((None, 2, row, 0, 2 * place + x))
                for k in range(1, line):
                    plan.append((place >= k, 2 + k, row, 0, 2 * (place - k) + x))
                    plan.append((place < k, 2 + line - 1 + line - k, row, 0, 2 * (place - k + line) + x))
            return plan

        a, b = attention("attention", heads, lengths, order, [queries, q_other] + gathered, q_plan, kv_plan)
        mine.append(a)
        theirs.append(lax.ppermute(b, "seq", swap))
    return assemble(pair, mine, theirs)


def hold(arrays, others=(), token=False):
    count = len(arrays)
    hbm = pl.BlockSpec(memory_space=pltpu.HBM)
    return pl.pallas_call(
        lambda *refs: None,
        out_shape=[jax.ShapeDtypeStruct(array.shape, array.dtype) for array in arrays]
        + [jax.ShapeDtypeStruct((16, 128), jnp.bfloat16)] * token,
        in_specs=[hbm] * (count + len(others)),
        out_specs=[hbm] * (count + token),
        input_output_aliases={i: i for i in range(count)},
        compiler_params=pltpu.CompilerParams(vmem_limit_bytes=VMEM_BYTES),
        name="hold",
    )(*arrays, *others)


def short_shards(queries, keys, values, lengths, order):
    pair = lax.axis_index("seq") % 2
    n = queries.shape[0]
    parts = lax.axis_size("dp")
    both = ("dp", "seq")

    def permutation(links):
        return [(8 * d + 2 * a + x, 8 * d + 2 * b + x) for d in range(parts) for a, b in links for x in range(2)]

    across = [(8 * d + i, 8 * d + (i ^ 1)) for d in range(parts) for i in range(8)]
    outer = permutation([(z, z ^ 1) for z in range(4)])
    ends = permutation([(z, z ^ 3) for z in range(4)])

    def swap_x(a):
        return lax.ppermute(a, both, across)

    def swap_outer(a):
        return lax.ppermute(a, both, outer)

    def swap_ends(a):
        return lax.ppermute(a, both, ends)

    def rows(*blocks):
        return jnp.concatenate(blocks, axis=0)

    def near(place):
        return place + 1 - 2 * (place % 2)

    one, two = HEAD_DIM, 2 * HEAD_DIM
    kv_half, q_half = KV_HALF * HEAD_DIM, KV_HALF * GQ

    def kv_plan(pair):
        t = [[(a, half * kv_half, two) for a in range(2)] for half in (pair, 1 - pair)]
        w = [
            [(a, half * kv_half + head * one, one) for head in (2, 3) for a in range(2)] for half in (pair, 1 - pair)
        ]
        return t + w

    def q_plan(pair):
        return [[(0, (1 - pair) * q_half + i * 2 * GQ, 2 * GQ)] for i in range(2)]

    t_own, t_send, w_own, w_send = split("split_kv", [keys, values], [2 * two] * 4, kv_plan)
    t_par = swap_x(t_send)
    t_near_own, t_far_own = swap_outer(t_own), swap_ends(t_own)
    w_par = swap_x(w_send)
    t_near_par, t_far_par = swap_outer(t_par), swap_ends(t_par)
    t_out_own = swap_outer(t_far_own)
    qt_send, qw_send = split("split_q", [queries], [2 * GQ] * 2, q_plan, [w_par])
    qt_par, qw_par = swap_x(qt_send), swap_x(qw_send)
    t_out_par = swap_outer(t_far_par)
    (u_shard,) = hold([rows(w_own[:, :two], w_par[:, :two])], [t_far_par])
    v_shard = rows(w_own[:, two:], w_par[:, two:])
    u_far = swap_ends(u_shard)
    u_near, u_out = swap_outer(u_shard), swap_outer(u_far)
    v_far = swap_ends(v_shard)
    v_near, v_out = swap_outer(v_shard), swap_outer(v_far)

    def each_half(plan):
        def full(place, pair):
            return [
                (condition, array, row, column, 2 * owner + x)
                for half, x in enumerate((pair, 1 - pair))
                for condition, array, row, column, owner in plan(place, half)
            ]

        return full

    def t_queries(place, pair):
        return [(1, 0, 0, 2 * place + 1 - pair), (0, 0, pair * q_half, 2 * place + pair)]

    def t_keys(place, half):
        return [
            (None, 2 + half, 0, 0, place),
            (None, 4 + half, 0, 0, near(place)),
            (None, 6 + half, 0, 0, 3 - place),
            (None, 8 + half, 0, 0, 3 - near(place)),
        ]

    t_other, wide = attention(
        "attention_t",
        2,
        lengths,
        order,
        [queries, qt_par, t_own, t_par, t_near_own, t_near_par, t_far_own, t_far_par, t_out_own, t_out_par],
        t_queries,
        each_half(t_keys),
        column=lambda pair: pair * q_half,
    )
    t_theirs = swap_x(t_other)


    def w_queries(head):
        def own(place, pair):
            return [(0, 0, pair * q_half + head * GQ, 2 * place + pair)]

        def other(place, pair):
            return [(1, 0, (head - 2) * GQ, 2 * place + 1 - pair)]

        return own, other, lambda place, pair: other(place, pair) + own(place, pair)

    def w_keys(place, half):
        return [
            (None, 2, half * n, 0, place),
            (None, 3, half * n, 0, near(place)),
            (None, 4, half * n, 0, 3 - place),
            (None, 5, half * n, 0, 3 - near(place)),
        ]

    u_other, wide = attention(
        "attention_u",
        1,
        lengths,
        order,
        [queries, qw_par, u_shard, u_near, u_far, u_out],
        w_queries(2)[2],
        each_half(w_keys),
        wide=wide,
        column=lambda pair: pair * q_half + 2 * GQ,
    )
    u_theirs = swap_x(u_other)
    theirs = (1 - pair) * q_half
    wide = lax.dynamic_update_slice_in_dim(wide, t_theirs, theirs, 1)
    v_arrays = [queries, qw_par, v_shard, v_near, v_far, v_out]
    (v_other,) = attention(
        "attention_v_other", 1, lengths, order, v_arrays + [u_other], w_queries(3)[1], each_half(w_keys)
    )
    v_theirs = swap_x(v_other)
    (wide,) = attention(
        "attention_v_own",
        1,
        lengths,
        order,
        v_arrays + [v_other],
        w_queries(3)[0],
        each_half(w_keys),
        wide=wide,
        column=lambda pair: pair * q_half + 3 * GQ,
    )
    wide = lax.dynamic_update_slice_in_dim(wide, u_theirs, theirs + 2 * GQ, 1)
    return lax.dynamic_update_slice_in_dim(wide, v_theirs, theirs + 3 * GQ, 1)


def shards(queries, keys, values, lengths, order):
    whole = short_shards if lax.axis_size("seq") == 8 else line_shards
    return whole(queries, keys, values, lengths, order)


def solution(mesh):
    placed = (
        P(("dp", "seq"), None),
        P(("dp", "seq"), None),
        P(("dp", "seq"), None),
        P("dp"),
        P("dp"),
    )
    return jax.shard_map(
        shards, mesh=mesh, in_specs=placed, out_specs=P(("dp", "seq"), None), check_vma=False
    )
```
